256 devices in a mesh: row: 64 (over y, x_lo, z), col: 4 (over x_hi, core).
Axes of the slice: x: 4 (x_hi: 2, x_lo: 2; x = x_hi * 2 + x_lo), y: 4, z: 8, core: 2. Of those that a mesh axis runs over, the one named last changes fastest.
Arguments:
- amplitudes: bfloat16 [128, 1024, 1200], P(None, 'row', 'col'), may hold values from -16 to 16
- integrals: bfloat16 [128, 1200, 4800], P('row', None, 'col'), may hold values from -0.046875 to 0.046875
- occupied_irrep: int32 [128], replicated, may hold values from 0 to 7
- virtual_irrep: int32 [1200], replicated, may hold values from 0 to 7, as said below
- occupied_energy: float32 [128], replicated, may hold values from -1.2 to -0.3
- virtual_energy: float32 [1200], replicated, may hold values from 0.1 to 1.5
- residual_in: float32 [1024, 4800], P('row', 'col'), may hold values from -6 to 6
Outputs:
- update: float32 [1024, 4800], P('row', 'col')
The draws below stay inside these ranges and needn't reach their ends.
Inputs may be any that keep to these rules, and one draw needn't show every extreme that they name: `occupied_irrep`: D2h irrep labels. `virtual_irrep`: D2h irrep labels, never decreasing along the orbitals; each label is held by 1 to 200 orbitals, one label by exactly 200.
All inputs are finite; a program needn't handle non-finite values.
Results may differ from the reference program's by a relative error of at most 0.0003.
Values may be sent and summed in bfloat16 or wider, within the bound.
No kernel may reach another device: no remote copies, remote signals or barrier semaphores. Data moves between devices by JAX's collectives and lax.ppermute only.
A program may use at most 64 MiB of HBM per device.

```python
import jax
import jax.numpy as jnp
from jax import lax

O_WIN = 128
A_WIN = 1024
V = 1200
CAPV = 200
NJ = 4


def draw_virtual_irrep(key, part):
    key = jax.random.fold_in(key, 11)
    first_key, second_key = jax.random.split(key, 2)
    remain = V - CAPV
    base_count = remain // 7
    leftover = remain - 7 * base_count
    spread = max(1, base_count // 4)
    wobble = jax.random.randint(first_key, (7,), 0, spread).astype(jnp.int32)
    others = base_count + wobble - jnp.roll(wobble, 1)
    others = others + jnp.concatenate([jnp.array([leftover], jnp.int32), jnp.zeros((6,), jnp.int32)])
    biggest = jax.random.randint(second_key, (), 0, 8).astype(jnp.int32)
    labels_all = jnp.arange(8, dtype=jnp.int32)
    lower = others[jnp.clip(labels_all, 0, 6)]
    upper = others[jnp.clip(labels_all - 1, 0, 6)]
    counts = jnp.where(labels_all < biggest, lower, jnp.where(labels_all == biggest, CAPV, upper)).astype(jnp.int32)
    ends = jnp.cumsum(counts).astype(jnp.int32)
    orbital = jnp.arange(V, dtype=jnp.int32)
    return jnp.sum((orbital[:, None] >= ends[None, :]).astype(jnp.int32), axis=1).astype(jnp.int32)


def plant(result, rng, smallest, top_value):
    longest = result.shape.index(max(result.shape))
    spots = []
    for shift in (0, 1):
        where = [jax.random.randint(jax.random.fold_in(rng, axis), (), 0, length) for axis, length in enumerate(result.shape)]
        where[longest] = (where[longest] + shift) % result.shape[longest]
        spots.append(tuple(where))
    return result.at[spots[0]].set(smallest).at[spots[1]].set(top_value)


def spiked(result, key, source, target, parts, factor):
    owner, partner = [(jnp.arange(result.shape[position]) // (result.shape[position] // parts)).reshape([-1 if axis == position else 1 for axis in range(result.ndim)]) for position in (source, target)]
    chosen = jax.random.permutation(key, parts)[partner]
    strong = (owner == chosen) | (owner == (partner + parts // 2) % parts)
    return jnp.where(strong, factor * result, result)


def levels(rng, extent, shards, smallest, top_value):
    def one(dim, shards_of):
        draws = jax.random.uniform(jax.random.fold_in(jax.random.fold_in(rng, 6), dim), (shards_of,), jnp.float32, smallest / len(shards), top_value / len(shards))
        return jnp.repeat(jnp.exp(draws), extent[dim] // shards_of).reshape((-1,) + (1,) * (len(extent) - dim - 1))

    factor_of = one(*shards[0])
    for cut in shards[1:]:
        factor_of = factor_of * one(*cut)
    return factor_of


def gaussian(rng, dims, scale, most, cuts=(), held_as=jnp.bfloat16):
    level = levels(rng, dims, cuts, -0.22, 0.18) if cuts else 1.0
    values = jax.random.normal(rng, dims, jnp.float32) * scale * level
    return jnp.minimum(jnp.maximum(values, -most), most).astype(held_as)


def heavy_noise(stream_key, shape, scale, bound, cuts, heavy, held_as=jnp.bfloat16):
    result = scale * jax.random.normal(stream_key, shape, jnp.float32)
    if cuts:
        result = result * levels(stream_key, shape, cuts, -0.22, 0.18)
    return jnp.clip(spiked(result, jax.random.fold_in(stream_key, 3), *heavy), -bound, bound).astype(held_as)


def setup_inputs(seed: int = 0) -> dict:
    key_of = jax.random.split(jax.random.key(seed), 8)
    return {
        "amplitudes": heavy_noise(key_of[0], (O_WIN, A_WIN, V), 1.0, 16.0, ((1, 64), (2, 4)), (0, 1, 64, 4.0)),
        "integrals": gaussian(key_of[1], (O_WIN, V, NJ * V), (O_WIN * V // 8) ** -0.5, 0.046875, ((0, 64), (2, 4))),
        "occupied_irrep": plant(jax.random.randint(key_of[2], (O_WIN,), 0, 8), jax.random.fold_in(key_of[2], 1), 0, 7).astype(jnp.int32),
        "virtual_irrep": draw_virtual_irrep(jax.random.fold_in(key_of[7], 71), 0),
        "occupied_energy": jnp.clip(jax.random.uniform(key_of[4], (O_WIN,), jnp.float32, -1.2, -0.3), -1.2, -0.3),
        "virtual_energy": jnp.clip(jax.random.uniform(key_of[5], (V,), jnp.float32, 0.1, 1.5), 0.1, 1.5),
        "residual_in": gaussian(key_of[6], (A_WIN, NJ * V), 1.0, 6.0, ((0, 64), (1, 4)), jnp.float32),
    }


def reference(amplitudes, integrals, occupied_irrep, virtual_irrep, occupied_energy, virtual_energy, residual_in):
    a_labels = virtual_irrep[:A_WIN]
    jb_labels = jnp.bitwise_xor(occupied_irrep[1:1 + NJ][:, None], virtual_irrep[None, :]).reshape(-1)
    i_label = occupied_irrep[0]

    def add_orbital(total, item):
        amp_row, int_row, k_label = item
        keep_amp = jnp.bitwise_xor(jnp.bitwise_xor(i_label, k_label), jnp.bitwise_xor(a_labels[:, None], virtual_irrep[None, :])) == 0
        sym_amp = jnp.where(keep_amp, amp_row, jnp.zeros_like(amp_row))
        keep_int = jnp.bitwise_xor(jnp.bitwise_xor(k_label, virtual_irrep[:, None]), jb_labels[None, :]) == 0
        sym_int = jnp.where(keep_int, int_row, jnp.zeros_like(int_row))
        return total + jnp.dot(sym_amp, sym_int, preferred_element_type=jnp.float32), None

    start_total = jnp.zeros((A_WIN, NJ * V), jnp.float32)
    cycle_term, _ = lax.scan(add_orbital, start_total, (amplitudes, integrals, occupied_irrep))
    energy_jb = (occupied_energy[1:1 + NJ][:, None] - virtual_energy[None, :]).reshape(-1)
    denominator = occupied_energy[0] - virtual_energy[:A_WIN][:, None] + energy_jb[None, :]
    return (residual_in + cycle_term) / denominator
```

```python
import functools

import jax
import jax.numpy as jnp
from jax import lax
from jax.experimental import pallas as pl
from jax.experimental.pallas import tpu as pltpu
from jax.sharding import PartitionSpec as P

NJ = 4
FAR = 2
PARTNERS = (0, 48)
FOLD = 256
QUARTER = FOLD // 4
SEND_TYPE = jnp.float16
SEND_SCALE = 64.0


def colour(row):
    return (row >> 5) & 1


SAME = [row for row in range(64) if colour(row) == 0]


def own_shift():
    mine = colour(lax.axis_index("row"))
    shift = jnp.int32(0)
    for c in range(1, FAR):
        shift = jnp.where(mine == c, PARTNERS[c], shift)
    return shift


def fold_amplitudes(odd, amp_hbm, occ_vec_hbm, occ_hbm, vir_hbm, after_hbm, out_ref, amp_ref, occ_vec_ref, occ_ref, vir_ref, mask_ref, sems):
    cols, rows, occ = amp_ref.shape
    step = cols // (sems.shape[0] - 3)
    small = [
        pltpu.make_async_copy(vir_hbm, vir_ref, sems.at[0]),
        pltpu.make_async_copy(occ_hbm, occ_ref, sems.at[1]),
        pltpu.make_async_copy(occ_vec_hbm, occ_vec_ref, sems.at[2]),
    ]
    large = [
        pltpu.make_async_copy(amp_hbm.at[pl.ds(c, step)], amp_ref.at[pl.ds(c, step)], sems.at[3 + c // step])
        for c in range(0, cols, step)
    ]
    for copy in small + large:
        copy.start()
    for copy in small:
        copy.wait()
    me = lax.axis_index("col")
    first_a = lax.axis_index("row") * rows
    row_id = lax.broadcasted_iota(jnp.int32, (rows, occ), 0)
    a_labels = jnp.zeros((rows, occ), jnp.int32)
    for a in range(rows):
        a_labels = jnp.where(row_id == a, vir_ref[first_a + a], a_labels)
    wanted = occ_ref[0] ^ occ_vec_ref[...] ^ a_labels
    for label in range(8):
        mask_ref[label] = jnp.where(wanted == label, 1.0, 0.0).astype(jnp.bfloat16)
    def run(col, i):
        start = col * cols
        lo, end = i * step, (i + 1) * step
        while lo < end:
            slot = (start + lo) % FOLD
            hi = min(end, lo + QUARTER - slot % QUARTER, FOLD if lo < FOLD else end)
            p = (slot // QUARTER) ^ col
            first = slot % QUARTER
            again = lo >= FOLD
            if p % 2 != odd:
                lo = hi
                continue

            def one(c, lo=lo, p=p, first=first, again=again):
                x = amp_ref[c] * mask_ref[vir_ref[start + c]]
                place = c - lo + first
                if again:
                    x = x + out_ref[p // 2, place]
                out_ref[p // 2, place] = x

            unit = 10
            whole = (hi - lo) // unit * unit

            def body(n, carry, lo=lo, one=one):
                for u in range(unit):
                    one(lo + n * unit + u)
                return carry

            lax.fori_loop(0, whole // unit, body, 0)
            for c in range(lo + whole, hi):
                one(c)
            lo = hi

    for i, copy in enumerate(large):
        copy.wait()
        for col in range(4):

            @pl.when(me == col)
            def _(col=col, i=i):
                run(col, i)


def turn_amplitudes(a_ref, b_ref, c_ref, out_ref, rows_ref, turned_ref):
    _, slots, rows, occ = a_ref.shape
    total = a_ref[0] + b_ref[0] + c_ref[...]
    rows_ref[...] = total.astype(jnp.float32).reshape(slots * rows, occ)
    half = occ // 2
    to = lax.broadcasted_iota(jnp.int32, (occ, occ), 0)
    frm = lax.broadcasted_iota(jnp.int32, (occ, occ), 1)
    pick = (frm == 2 * (to % half) + to // half).astype(jnp.bfloat16)
    for a in range(rows):
        block = rows_ref[pl.ds(a, slots, stride=rows), :].astype(jnp.bfloat16)
        turned = lax.dot_general(pick, block, (((1,), (1,)), ((), ())), preferred_element_type=jnp.float32)
        turned_ref[pl.ds(a, half, stride=rows), :] = jnp.concatenate([turned[:half], turned[half:]], axis=1)
    shift = own_shift()
    for i, member in enumerate(SAME):
        for d, partner in enumerate(PARTNERS):
            row = (member ^ partner) ^ shift
            out_ref[i, d] = turned_ref[pl.ds(pl.multiple_of(row * rows, rows), rows), :].astype(jnp.bfloat16)


def fold_integrals(int_hbm, occ_hbm, vir_hbm, after_hbm, out_ref, lab_ref, vec_ref, int_ref, occ_ref, vir_ref, small, sems):
    _, v, width = int_ref.shape
    near = [pltpu.make_async_copy(vir_hbm, vir_ref, small.at[0]), pltpu.make_async_copy(occ_hbm, occ_ref, small.at[1])]
    step = v // sems.shape[1]
    copies = [
        [
            pltpu.make_async_copy(int_hbm.at[k, pl.ds(c, step)], int_ref.at[k, pl.ds(c, step)], sems.at[k, c // step])
            for c in range(0, v, step)
        ]
        for k in range(2)
    ]
    for copy in near + copies[0] + copies[1]:
        copy.start()
    for copy in near:
        copy.wait()
    begins = []
    for label in range(1, 8):
        lo, hi = jnp.int32(0), jnp.int32(v)
        for _ in range(v.bit_length()):
            mid = jnp.minimum((lo + hi) // 2, v - 1)
            reached = vir_ref[mid] >= label
            lo, hi = jnp.where(reached, lo, mid + 1), jnp.where(reached, mid, hi)
        begins.append(hi)

    def labels_of(orbital):
        return sum((orbital >= begin).astype(jnp.int32) for begin in begins)

    for c in range(0, v, 80):
        at = lax.broadcasted_iota(jnp.int32, (80, 128), 0) + c
        lab_ref[c : c + 80, :] = labels_of(at).astype(jnp.bfloat16)
    vir_vec = labels_of(lax.broadcasted_iota(jnp.int32, (1, width), 1))
    vec_ref[...] = vir_vec
    for k in range(2):
        label = occ_ref[lax.axis_index("row") * 2 + k] ^ occ_ref[1 + lax.axis_index("col")]
        b_labels = (vir_vec ^ label).astype(jnp.bfloat16)
        for i, copy in enumerate(copies[k]):
            copy.wait()
            for c in range(i * step, (i + 1) * step, 80):
                rows = slice(c, c + 80)
                c_labels = lab_ref[rows, :]
                for n in range(FOLD // 128):
                    total = None
                    for b in range(n * 128, width, FOLD):
                        size = min(128, width - b)
                        x = int_ref[k, rows, b : b + size]
                        x = jnp.where(c_labels[:, :size] == b_labels[:, b : b + size], x, jnp.zeros_like(x))
                        if size < 128:
                            x = jnp.concatenate([x, jnp.zeros((80, 128 - size), x.dtype)], axis=1)
                        total = x if total is None else total + x
                    out_ref[k, rows, n * 128 : (n + 1) * 128] = total
        out_ref[k, v:, :] = jnp.zeros((out_ref.shape[1] - v, FOLD), out_ref.dtype)


def contract(terms, last, *refs):
    quarters, partners = sorted({p for p, _ in terms}), sorted({d for _, d in terms})
    cut = len(quarters) + len(partners)
    t_refs, w_refs = refs[: len(quarters)], refs[len(quarters) : cut]
    lab_ref, vec_ref, occ_ref = refs[cut : cut + 3]
    sum_refs, (out_ref, a_lab_ref) = refs[cut + 3 : -2], refs[-2:]
    near, far, rows, lanes = t_refs[0].shape
    v = vec_ref.shape[1]
    me = lax.axis_index("col")
    own = lax.axis_index("row")
    shift = own_shift()
    for i, member in enumerate(SAME):
        label = lab_ref[pl.ds(pl.multiple_of((member ^ shift) * rows, rows), rows), :]
        a_lab_ref[i * rows : (i + 1) * rows, :] = label
    high = lax.broadcasted_iota(jnp.int32, (1, lanes), 1) >= QUARTER

    def labels_at(c):
        x = vec_ref[:, c : min(c + QUARTER, v)]
        if c + QUARTER > v:
            x = jnp.concatenate([x, jnp.full((1, c + QUARTER - v), 64, jnp.int32)], axis=1)
        return jnp.concatenate([x, x], axis=1)

    for col in range(4):

        @pl.when(me == col)
        def _(col=col):
            total = sum_refs[0][...] if sum_refs else None
            a_labels = a_lab_ref[...]
            blocks = [(p, d, c) for p, d in terms for c in range((col ^ p) * QUARTER, v, FOLD)]
            for n in range(0, len(blocks), 2):
                lhs, w = [], []
                for p, d, c in blocks[n : n + 2]:
                    other = 2 * (own ^ PARTNERS[d])
                    wanted = jnp.where(high, occ_ref[other + 1], occ_ref[other]) ^ occ_ref[0]
                    x = t_refs[quarters.index(p)][:, d].reshape(near * rows, lanes)
                    c_labels = (labels_at(c) ^ wanted).astype(jnp.bfloat16)
                    lhs.append(jnp.where(a_labels == c_labels, x, jnp.zeros_like(x)))
                    w += [w_refs[partners.index(d)][k, c : c + QUARTER, :] for k in range(2)]
                lhs = lhs[0] if len(lhs) == 1 else jnp.concatenate(lhs, axis=1)
                part = jnp.dot(lhs, jnp.concatenate(w, axis=0), preferred_element_type=jnp.float32)
                total = part if total is None else total + part
            out_ref[...] = total * SEND_SCALE if last else total


def prepare(res_ref, vir_vec_ref, energy_vec_ref, occ_ref, vir_ref, occ_e_ref, vir_e_ref, plain_ref, factor_ref):
    rows, v = res_ref.shape
    first_a = lax.axis_index("row") * rows
    j = 1 + lax.axis_index("col")
    row_id = lax.broadcasted_iota(jnp.int32, (rows, 128), 0)
    a_labels = jnp.zeros((rows, 128), jnp.int32)
    a_energy = jnp.zeros((rows, 128), jnp.float32)
    for a in range(rows):
        a_labels = jnp.where(row_id == a, vir_ref[first_a + a], a_labels)
        a_energy = jnp.where(row_id == a, vir_e_ref[first_a + a], a_energy)
    b_labels = vir_vec_ref[...] ^ occ_ref[0] ^ occ_ref[j]
    for b in range(0, v, 128):
        width = min(128, v - b)
        at = slice(b, b + width)
        denominator = occ_e_ref[0] - a_energy[:, :width] + (occ_e_ref[j] - energy_vec_ref[:, at])
        plain_ref[:, at] = res_ref[:, at] / denominator
        factor_ref[:, at] = jnp.where(a_labels[:, :width] == b_labels[:, at], (1.0 / SEND_SCALE) / denominator, 0.0)


def finish(part_ref, plain_ref, factor_ref, out_ref):
    total = part_ref[...]
    v = out_ref.shape[1]
    for b in range(0, v, FOLD):
        width = min(FOLD, v - b)
        at = slice(b, b + width)
        out_ref[:, at] = plain_ref[:, at] + factor_ref[:, at] * total[:, :width]


def local(
    amplitudes,
    integrals,
    occupied_irrep,
    virtual_irrep,
    occupied_energy,
    virtual_energy,
    residual_in,
):
    o_win, rows, cols = amplitudes.shape
    occ_local, v, n_local = integrals.shape
    n_row = o_win // occ_local
    near = n_row // FAR
    smem = pl.BlockSpec(memory_space=pltpu.SMEM)
    vmem = pl.BlockSpec(memory_space=pltpu.VMEM)
    hbm = pl.BlockSpec(memory_space=pltpu.HBM)
    big = pltpu.CompilerParams(vmem_limit_bytes=24 * 1024 * 1024)
    occ_vec = occupied_irrep.reshape(1, o_win)

    chunks = 6
    def folded(odd, after):
        return pl.pallas_call(
            functools.partial(fold_amplitudes, odd),
            out_shape=jax.ShapeDtypeStruct((2, QUARTER, rows, o_win), jnp.bfloat16),
            in_specs=[hbm] * 5,
            out_specs=vmem,
            scratch_shapes=[
                pltpu.VMEM((cols, rows, o_win), jnp.bfloat16),
                pltpu.VMEM((1, o_win), jnp.int32),
                pltpu.SMEM((o_win,), jnp.int32),
                pltpu.SMEM((v,), jnp.int32),
                pltpu.VMEM((8, rows, o_win), jnp.bfloat16),
                pltpu.SemaphoreType.DMA((3 + chunks,)),
            ],
            compiler_params=big,
            name="fold_amplitudes",
        )(
            pltpu.with_memory_space_constraint(amplitudes.transpose(2, 1, 0), pltpu.HBM),
            pltpu.with_memory_space_constraint(occ_vec, pltpu.HBM),
            pltpu.with_memory_space_constraint(occupied_irrep, pltpu.HBM),
            pltpu.with_memory_space_constraint(virtual_irrep, pltpu.HBM),
            after,
        )

    send = folded(1, pltpu.with_memory_space_constraint(occupied_irrep, pltpu.HBM))
    keep = folded(0, send)

    def swap(x, p):
        return lax.ppermute(x, "col", [(m, m ^ p) for m in range(4)])

    got = swap(send, 1)
    passed = keep[1] + got[1]
    w, labels, vir_vec = pl.pallas_call(
        fold_integrals,
        out_shape=[
            jax.ShapeDtypeStruct((occ_local, -(-v // QUARTER) * QUARTER, FOLD), jnp.bfloat16),
            jax.ShapeDtypeStruct((v, 128), jnp.bfloat16),
            jax.ShapeDtypeStruct((1, v), jnp.int32),
        ],
        in_specs=[hbm] * 4,
        out_specs=[vmem] * 3,
        scratch_shapes=[
            pltpu.VMEM((occ_local, v, n_local), jnp.bfloat16),
            pltpu.SMEM((o_win,), jnp.int32),
            pltpu.SMEM((v,), jnp.int32),
            pltpu.SemaphoreType.DMA((2,)),
            pltpu.SemaphoreType.DMA((occ_local, 5)),
        ],
        compiler_params=big,
        name="fold_integrals",
    )(
        pltpu.with_memory_space_constraint(integrals, pltpu.HBM),
        pltpu.with_memory_space_constraint(occupied_irrep, pltpu.HBM),
        pltpu.with_memory_space_constraint(virtual_irrep, pltpu.HBM),
        passed,
    )
    far = swap(passed, 2)
    turned = pl.pallas_call(
        turn_amplitudes,
        out_shape=jax.ShapeDtypeStruct((near, FAR, rows, occ_local * QUARTER), jnp.bfloat16),
        in_specs=[vmem] * 3,
        out_specs=vmem,
        scratch_shapes=[
            pltpu.VMEM((QUARTER * rows, o_win), jnp.float32),
            pltpu.VMEM((n_row * rows, o_win), jnp.float32),
        ],
        compiler_params=big,
        cost_estimate=pl.CostEstimate(flops=4 * 10**10, bytes_accessed=10**6, transcendentals=0),
        name="turn_amplitudes",
    )(keep, got, far)
    classes = [[member ^ partner for member in SAME] for partner in PARTNERS]
    mine = lax.all_to_all(turned, "row", split_axis=0, concat_axis=0, tiled=True, axis_index_groups=classes)
    across = swap(mine, 2)

    gathered = [w, lax.ppermute(w, "row", [(r, r ^ PARTNERS[1]) for r in range(n_row)])]
    quarters = [mine, swap(mine, 1), across, swap(across, 1)]

    def contracted(terms, last, sums):
        used = [quarters[p] for p in sorted({p for p, _ in terms})] + [gathered[d] for d in sorted({d for _, d in terms})]
        return pl.pallas_call(
            functools.partial(contract, terms, last),
            out_shape=jax.ShapeDtypeStruct((near * rows, FOLD), jnp.float32),
            in_specs=[vmem] * (len(used) + 2) + [smem] + [vmem] * len(sums),
            out_specs=vmem,
            scratch_shapes=[pltpu.VMEM((near * rows, occ_local * QUARTER), jnp.bfloat16)],
            compiler_params=big,
            name="contract",
        )(*used, labels, vir_vec, occupied_irrep, *sums)

    early = [(0, 0), (1, 0), (2, 0)]
    partial = contracted(early, False, [])
    partial = contracted([(0, 1), (1, 1), (2, 1), (3, 0), (3, 1)], True, [partial])
    parts = lax.all_to_all(
        partial.astype(SEND_TYPE).reshape(near, rows, FOLD),
        "row",
        split_axis=0,
        concat_axis=0,
        tiled=True,
        axis_index_groups=classes,
    )
    plain, factor = pl.pallas_call(
        prepare,
        out_shape=[jax.ShapeDtypeStruct(residual_in.shape, jnp.float32)] * 2,
        in_specs=[vmem] * 3 + [smem] * 4,
        out_specs=[vmem, vmem],
        compiler_params=big,
        name="prepare",
    )(
        residual_in,
        vir_vec,
        virtual_energy.reshape(1, v),
        occupied_irrep,
        virtual_irrep,
        occupied_energy,
        virtual_energy,
    )
    return pl.pallas_call(
        finish,
        out_shape=jax.ShapeDtypeStruct(residual_in.shape, jnp.float32),
        in_specs=[vmem] * 3,
        out_specs=vmem,
        compiler_params=big,
        name="finish",
    )(jnp.sum(parts.astype(jnp.float32), axis=0), plain, factor)


def solution(mesh):
    in_specs = (P(None, "row", "col"), P("row", None, "col"), P(), P(), P(), P(), P("row", "col"))
    out_specs = P("row", "col")
    return jax.shard_map(local, mesh=mesh, in_specs=in_specs, out_specs=out_specs, check_vma=False)
```

```python
import functools

import jax
import jax.numpy as jnp
from jax import lax
from jax.experimental import pallas as pl
from jax.experimental.pallas import tpu as pltpu
from jax.sharding import PartitionSpec as P

NJ = 4
FAR = 2
PARTNERS = (0, 48)
FOLD = 256
QUARTER = FOLD // 4
SEND_TYPE = jnp.float16
SEND_SCALE = 64.0


def colour(row):
    return (row >> 5) & 1


SAME = sorted((row for row in range(64) if colour(row) == 0), key=lambda row: (row & 7, row >> 3))


def own_shift():
    mine = colour(lax.axis_index("row"))
    shift = jnp.int32(0)
    for c in range(1, FAR):
        shift = jnp.where(mine == c, PARTNERS[c], shift)
    return shift


def fold_amplitudes(odd, amp_hbm, occ_vec_hbm, occ_hbm, vir_hbm, after_hbm, out_ref, amp_ref, occ_vec_ref, occ_ref, vir_ref, mask_ref, sems):
    cols, rows, occ = amp_ref.shape
    step = cols // (sems.shape[0] - 3)
    small = [
        pltpu.make_async_copy(vir_hbm, vir_ref, sems.at[0]),
        pltpu.make_async_copy(occ_hbm, occ_ref, sems.at[1]),
        pltpu.make_async_copy(occ_vec_hbm, occ_vec_ref, sems.at[2]),
    ]
    large = [
        pltpu.make_async_copy(amp_hbm.at[pl.ds(c, step)], amp_ref.at[pl.ds(c, step)], sems.at[3 + c // step])
        for c in range(0, cols, step)
    ]
    for copy in small + large:
        copy.start()
    for copy in small:
        copy.wait()
    me = lax.axis_index("col")
    first_a = lax.axis_index("row") * rows
    row_id = lax.broadcasted_iota(jnp.int32, (rows, occ), 0)
    a_labels = jnp.zeros((rows, occ), jnp.int32)
    for a in range(rows):
        a_labels = jnp.where(row_id == a, vir_ref[first_a + a], a_labels)
    wanted = occ_ref[0] ^ occ_vec_ref[...] ^ a_labels
    for label in range(8):
        mask_ref[label] = jnp.where(wanted == label, 1.0, 0.0).astype(jnp.bfloat16)
    def run(col, i):
        start = col * cols
        lo, end = i * step, (i + 1) * step
        while lo < end:
            slot = (start + lo) % FOLD
            hi = min(end, lo + QUARTER - slot % QUARTER, FOLD if lo < FOLD else end)
            p = (slot // QUARTER) ^ col
            first = slot % QUARTER
            again = lo >= FOLD
            if p % 2 != odd:
                lo = hi
                continue

            def one(c, lo=lo, p=p, first=first, again=again):
                x = amp_ref[c] * mask_ref[vir_ref[start + c]]
                place = c - lo + first
                if again:
                    x = x + out_ref[p // 2, place]
                out_ref[p // 2, place] = x

            unit = 10
            whole = (hi - lo) // unit * unit

            def body(n, carry, lo=lo, one=one):
                for u in range(unit):
                    one(lo + n * unit + u)
                return carry

            lax.fori_loop(0, whole // unit, body, 0)
            for c in range(lo + whole, hi):
                one(c)
            lo = hi

    for i, copy in enumerate(large):
        copy.wait()
        for col in range(4):

            @pl.when(me == col)
            def _(col=col, i=i):
                run(col, i)


def turn_amplitudes(a_ref, b_ref, c_ref, out_ref, rows_ref, turned_ref):
    _, slots, rows, occ = a_ref.shape
    total = a_ref[0] + b_ref[0] + c_ref[...]
    rows_ref[...] = total.astype(jnp.float32).reshape(slots * rows, occ)
    half = occ // 2
    to = lax.broadcasted_iota(jnp.int32, (occ, occ), 0)
    frm = lax.broadcasted_iota(jnp.int32, (occ, occ), 1)
    pick = (frm == 2 * (to % half) + to // half).astype(jnp.bfloat16)
    for a in range(rows):
        block = rows_ref[pl.ds(a, slots, stride=rows), :].astype(jnp.bfloat16)
        turned = lax.dot_general(pick, block, (((1,), (1,)), ((), ())), preferred_element_type=jnp.float32)
        turned_ref[pl.ds(a, half, stride=rows), :] = jnp.concatenate([turned[:half], turned[half:]], axis=1)
    shift = own_shift()
    for i, member in enumerate(SAME):
        for d, partner in enumerate(PARTNERS):
            row = (member ^ partner) ^ shift
            out_ref[i, d] = turned_ref[pl.ds(pl.multiple_of(row * rows, rows), rows), :].astype(jnp.bfloat16)


def fold_integrals(int_hbm, occ_hbm, vir_hbm, after_hbm, out_ref, lab_ref, vec_ref, int_ref, occ_ref, vir_ref, small, sems):
    _, v, width = int_ref.shape
    near = [pltpu.make_async_copy(vir_hbm, vir_ref, small.at[0]), pltpu.make_async_copy(occ_hbm, occ_ref, small.at[1])]
    step = v // sems.shape[1]
    copies = [
        [
            pltpu.make_async_copy(int_hbm.at[k, pl.ds(c, step)], int_ref.at[k, pl.ds(c, step)], sems.at[k, c // step])
            for c in range(0, v, step)
        ]
        for k in range(2)
    ]
    for copy in near + copies[0] + copies[1]:
        copy.start()
    for copy in near:
        copy.wait()
    begins = []
    for label in range(1, 8):
        lo, hi = jnp.int32(0), jnp.int32(v)
        for _ in range(v.bit_length()):
            mid = jnp.minimum((lo + hi) // 2, v - 1)
            reached = vir_ref[mid] >= label
            lo, hi = jnp.where(reached, lo, mid + 1), jnp.where(reached, mid, hi)
        begins.append(hi)

    def labels_of(orbital):
        return sum((orbital >= begin).astype(jnp.int32) for begin in begins)

    for c in range(0, v, 80):
        at = lax.broadcasted_iota(jnp.int32, (80, 128), 0) + c
        lab_ref[c : c + 80, :] = labels_of(at).astype(jnp.bfloat16)
    vir_vec = labels_of(lax.broadcasted_iota(jnp.int32, (1, width), 1))
    vec_ref[...] = vir_vec
    for k in range(2):
        label = occ_ref[lax.axis_index("row") * 2 + k] ^ occ_ref[1 + lax.axis_index("col")]
        b_labels = (vir_vec ^ label).astype(jnp.bfloat16)
        for i, copy in enumerate(copies[k]):
            copy.wait()
            for c in range(i * step, (i + 1) * step, 80):
                rows = slice(c, c + 80)
                c_labels = lab_ref[rows, :]
                for n in range(FOLD // 128):
                    total = None
                    for b in range(n * 128, width, FOLD):
                        size = min(128, width - b)
                        x = int_ref[k, rows, b : b + size]
                        x = jnp.where(c_labels[:, :size] == b_labels[:, b : b + size], x, jnp.zeros_like(x))
                        if size < 128:
                            x = jnp.concatenate([x, jnp.zeros((80, 128 - size), x.dtype)], axis=1)
                        total = x if total is None else total + x
                    out_ref[k, rows, n * 128 : (n + 1) * 128] = total
        out_ref[k, v:, :] = jnp.zeros((out_ref.shape[1] - v, FOLD), out_ref.dtype)


def contract(terms, last, *refs):
    quarters, partners = sorted({p for p, _ in terms}), sorted({d for _, d in terms})
    cut = len(quarters) + len(partners)
    t_refs, w_refs = refs[: len(quarters)], refs[len(quarters) : cut]
    lab_ref, vec_ref, occ_ref = refs[cut : cut + 3]
    sum_refs, (out_ref, a_lab_ref) = refs[cut + 3 : -2], refs[-2:]
    near, far, rows, lanes = t_refs[0].shape
    v = vec_ref.shape[1]
    me = lax.axis_index("col")
    own = lax.axis_index("row")
    shift = own_shift()
    for i, member in enumerate(SAME):
        label = lab_ref[pl.ds(pl.multiple_of((member ^ shift) * rows, rows), rows), :]
        a_lab_ref[i * rows : (i + 1) * rows, :] = label
    high = lax.broadcasted_iota(jnp.int32, (1, lanes), 1) >= QUARTER

    def labels_at(c):
        x = vec_ref[:, c : min(c + QUARTER, v)]
        if c + QUARTER > v:
            x = jnp.concatenate([x, jnp.full((1, c + QUARTER - v), 64, jnp.int32)], axis=1)
        return jnp.concatenate([x, x], axis=1)

    for col in range(4):

        @pl.when(me == col)
        def _(col=col):
            total = sum_refs[0][...] if sum_refs else None
            a_labels = a_lab_ref[...]
            blocks = [(p, d, c) for p, d in terms for c in range((col ^ p) * QUARTER, v, FOLD)]
            for n in range(0, len(blocks), 2):
                lhs, w = [], []
                for p, d, c in blocks[n : n + 2]:
                    other = 2 * (own ^ PARTNERS[d])
                    wanted = jnp.where(high, occ_ref[other + 1], occ_ref[other]) ^ occ_ref[0]
                    x = t_refs[quarters.index(p)][:, d].reshape(near * rows, lanes)
                    c_labels = (labels_at(c) ^ wanted).astype(jnp.bfloat16)
                    lhs.append(jnp.where(a_labels == c_labels, x, jnp.zeros_like(x)))
                    w += [w_refs[partners.index(d)][k, c : c + QUARTER, :] for k in range(2)]
                lhs = lhs[0] if len(lhs) == 1 else jnp.concatenate(lhs, axis=1)
                part = jnp.dot(lhs, jnp.concatenate(w, axis=0), preferred_element_type=jnp.float32)
                total = part if total is None else total + part
            out_ref[...] = total * SEND_SCALE if last else total


def prepare(res_ref, vir_vec_ref, energy_vec_ref, occ_ref, vir_ref, occ_e_ref, vir_e_ref, plain_ref, factor_ref):
    rows, v = res_ref.shape
    first_a = lax.axis_index("row") * rows
    j = 1 + lax.axis_index("col")
    row_id = lax.broadcasted_iota(jnp.int32, (rows, 128), 0)
    a_labels = jnp.zeros((rows, 128), jnp.int32)
    a_energy = jnp.zeros((rows, 128), jnp.float32)
    for a in range(rows):
        a_labels = jnp.where(row_id == a, vir_ref[first_a + a], a_labels)
        a_energy = jnp.where(row_id == a, vir_e_ref[first_a + a], a_energy)
    b_labels = vir_vec_ref[...] ^ occ_ref[0] ^ occ_ref[j]
    for b in range(0, v, 128):
        width = min(128, v - b)
        at = slice(b, b + width)
        denominator = occ_e_ref[0] - a_energy[:, :width] + (occ_e_ref[j] - energy_vec_ref[:, at])
        plain_ref[:, at] = res_ref[:, at] / denominator
        factor_ref[:, at] = jnp.where(a_labels[:, :width] == b_labels[:, at], (1.0 / SEND_SCALE) / denominator, 0.0)


def finish(part_ref, plain_ref, factor_ref, out_ref):
    total = part_ref[...]
    v = out_ref.shape[1]
    for b in range(0, v, FOLD):
        width = min(FOLD, v - b)
        at = slice(b, b + width)
        out_ref[:, at] = plain_ref[:, at] + factor_ref[:, at] * total[:, :width]


def local(
    amplitudes,
    integrals,
    occupied_irrep,
    virtual_irrep,
    occupied_energy,
    virtual_energy,
    residual_in,
):
    o_win, rows, cols = amplitudes.shape
    occ_local, v, n_local = integrals.shape
    n_row = o_win // occ_local
    near = n_row // FAR
    smem = pl.BlockSpec(memory_space=pltpu.SMEM)
    vmem = pl.BlockSpec(memory_space=pltpu.VMEM)
    hbm = pl.BlockSpec(memory_space=pltpu.HBM)
    big = pltpu.CompilerParams(vmem_limit_bytes=24 * 1024 * 1024)
    occ_vec = occupied_irrep.reshape(1, o_win)

    chunks = 6
    def folded(odd, after):
        return pl.pallas_call(
            functools.partial(fold_amplitudes, odd),
            out_shape=jax.ShapeDtypeStruct((2, QUARTER, rows, o_win), jnp.bfloat16),
            in_specs=[hbm] * 5,
            out_specs=vmem,
            scratch_shapes=[
                pltpu.VMEM((cols, rows, o_win), jnp.bfloat16),
                pltpu.VMEM((1, o_win), jnp.int32),
                pltpu.SMEM((o_win,), jnp.int32),
                pltpu.SMEM((v,), jnp.int32),
                pltpu.VMEM((8, rows, o_win), jnp.bfloat16),
                pltpu.SemaphoreType.DMA((3 + chunks,)),
            ],
            compiler_params=big,
            name="fold_amplitudes",
        )(
            pltpu.with_memory_space_constraint(amplitudes.transpose(2, 1, 0), pltpu.HBM),
            pltpu.with_memory_space_constraint(occ_vec, pltpu.HBM),
            pltpu.with_memory_space_constraint(occupied_irrep, pltpu.HBM),
            pltpu.with_memory_space_constraint(virtual_irrep, pltpu.HBM),
            after,
        )

    send = folded(1, pltpu.with_memory_space_constraint(occupied_irrep, pltpu.HBM))
    keep = folded(0, send)

    def swap(x, p):
        return lax.ppermute(x, "col", [(m, m ^ p) for m in range(4)])

    got = swap(send, 1)
    passed = keep[1] + got[1]
    w, labels, vir_vec = pl.pallas_call(
        fold_integrals,
        out_shape=[
            jax.ShapeDtypeStruct((occ_local, -(-v // QUARTER) * QUARTER, FOLD), jnp.bfloat16),
            jax.ShapeDtypeStruct((v, 128), jnp.bfloat16),
            jax.ShapeDtypeStruct((1, v), jnp.int32),
        ],
        in_specs=[hbm] * 4,
        out_specs=[vmem] * 3,
        scratch_shapes=[
            pltpu.VMEM((occ_local, v, n_local), jnp.bfloat16),
            pltpu.SMEM((o_win,), jnp.int32),
            pltpu.SMEM((v,), jnp.int32),
            pltpu.SemaphoreType.DMA((2,)),
            pltpu.SemaphoreType.DMA((occ_local, 5)),
        ],
        compiler_params=big,
        name="fold_integrals",
    )(
        pltpu.with_memory_space_constraint(integrals, pltpu.HBM),
        pltpu.with_memory_space_constraint(occupied_irrep, pltpu.HBM),
        pltpu.with_memory_space_constraint(virtual_irrep, pltpu.HBM),
        passed,
    )
    far = swap(passed, 2)
    turned = pl.pallas_call(
        turn_amplitudes,
        out_shape=jax.ShapeDtypeStruct((near, FAR, rows, occ_local * QUARTER), jnp.bfloat16),
        in_specs=[vmem] * 3,
        out_specs=vmem,
        scratch_shapes=[
            pltpu.VMEM((QUARTER * rows, o_win), jnp.float32),
            pltpu.VMEM((n_row * rows, o_win), jnp.float32),
        ],
        compiler_params=big,
        cost_estimate=pl.CostEstimate(flops=4 * 10**10, bytes_accessed=10**6, transcendentals=0),
        name="turn_amplitudes",
    )(keep, got, far)
    classes = [[member ^ partner for member in SAME] for partner in PARTNERS]
    mine = lax.all_to_all(turned, "row", split_axis=0, concat_axis=0, tiled=True, axis_index_groups=classes)
    across = swap(mine, 2)

    gathered = [w, lax.ppermute(w, "row", [(r, r ^ PARTNERS[1]) for r in range(n_row)])]
    quarters = [mine, swap(mine, 1), across, swap(across, 1)]

    def contracted(terms, last, sums):
        used = [quarters[p] for p in sorted({p for p, _ in terms})] + [gathered[d] for d in sorted({d for _, d in terms})]
        return pl.pallas_call(
            functools.partial(contract, terms, last),
            out_shape=jax.ShapeDtypeStruct((near * rows, FOLD), jnp.float32),
            in_specs=[vmem] * (len(used) + 2) + [smem] + [vmem] * len(sums),
            out_specs=vmem,
            scratch_shapes=[pltpu.VMEM((near * rows, occ_local * QUARTER), jnp.bfloat16)],
            compiler_params=big,
            name="contract",
        )(*used, labels, vir_vec, occupied_irrep, *sums)

    early = [(0, 0), (1, 0), (2, 0)]
    partial = contracted(early, False, [])
    partial = contracted([(0, 1), (1, 1), (2, 1), (3, 0), (3, 1)], True, [partial])
    parts = lax.all_to_all(
        partial.astype(SEND_TYPE).reshape(near, rows, FOLD),
        "row",
        split_axis=0,
        concat_axis=0,
        tiled=True,
        axis_index_groups=classes,
    )
    plain, factor = pl.pallas_call(
        prepare,
        out_shape=[jax.ShapeDtypeStruct(residual_in.shape, jnp.float32)] * 2,
        in_specs=[vmem] * 3 + [smem] * 4,
        out_specs=[vmem, vmem],
        compiler_params=big,
        name="prepare",
    )(
        residual_in,
        vir_vec,
        virtual_energy.reshape(1, v),
        occupied_irrep,
        virtual_irrep,
        occupied_energy,
        virtual_energy,
    )
    return pl.pallas_call(
        finish,
        out_shape=jax.ShapeDtypeStruct(residual_in.shape, jnp.float32),
        in_specs=[vmem] * 3,
        out_specs=vmem,
        compiler_params=big,
        name="finish",
    )(jnp.sum(parts.astype(jnp.float32), axis=0), plain, factor)


def solution(mesh):
    in_specs = (P(None, "row", "col"), P("row", None, "col"), P(), P(), P(), P(), P("row", "col"))
    out_specs = P("row", "col")
    return jax.shard_map(local, mesh=mesh, in_specs=in_specs, out_specs=out_specs, check_vma=False)
```

```python
import functools

import jax
import jax.numpy as jnp
from jax import lax
from jax.experimental import pallas as pl
from jax.experimental.pallas import tpu as pltpu
from jax.sharding import PartitionSpec as P

NJ = 4
FAR = 2
PARTNERS = (0, 48)
FOLD = 256
GROUP = 4
QUARTER = FOLD // 4
SEND_TYPE = jnp.float16
SEND_SCALE = 64.0


def colour(row):
    return (row >> 5) & 1


SAME = [row for row in range(64) if colour(row) == 0]


def own_shift():
    mine = colour(lax.axis_index("row"))
    shift = jnp.int32(0)
    for c in range(1, FAR):
        shift = jnp.where(mine == c, PARTNERS[c], shift)
    return shift


def fold_amplitudes(odd, amp_hbm, occ_vec_hbm, occ_hbm, vir_hbm, after_hbm, out_ref, amp_ref, occ_vec_ref, occ_ref, vir_ref, mask_ref, sems):
    cols, rows, occ = amp_ref.shape
    step = cols // (sems.shape[0] - 3)
    small = [
        pltpu.make_async_copy(vir_hbm, vir_ref, sems.at[0]),
        pltpu.make_async_copy(occ_hbm, occ_ref, sems.at[1]),
        pltpu.make_async_copy(occ_vec_hbm, occ_vec_ref, sems.at[2]),
    ]
    large = [
        pltpu.make_async_copy(amp_hbm.at[pl.ds(c, step)], amp_ref.at[pl.ds(c, step)], sems.at[3 + c // step])
        for c in range(0, cols, step)
    ]
    for copy in small + large:
        copy.start()
    for copy in small:
        copy.wait()
    me = lax.axis_index("col")
    first_a = lax.axis_index("row") * rows
    row_id = lax.broadcasted_iota(jnp.int32, (rows, occ), 0)
    a_labels = jnp.zeros((rows, occ), jnp.int32)
    for a in range(rows):
        a_labels = jnp.where(row_id == a, vir_ref[first_a + a], a_labels)
    wanted = occ_ref[0] ^ occ_vec_ref[...] ^ a_labels
    for label in range(8):
        mask_ref[label] = jnp.where(wanted == label, 1.0, 0.0).astype(jnp.bfloat16)
    def run(col, i):
        start = col * cols
        lo, end = i * step, (i + 1) * step
        while lo < end:
            slot = (start + lo) % FOLD
            hi = min(end, lo + QUARTER - slot % QUARTER, FOLD if lo < FOLD else end)
            p = (slot // QUARTER) ^ col
            first = slot % QUARTER
            again = lo >= FOLD
            if p % 2 != odd:
                lo = hi
                continue

            def one(c, lo=lo, p=p, first=first, again=again):
                x = amp_ref[c] * mask_ref[vir_ref[start + c]]
                place = c - lo + first
                if again:
                    x = x + out_ref[p // 2, place]
                out_ref[p // 2, place] = x

            unit = 10
            whole = (hi - lo) // unit * unit

            def body(n, carry, lo=lo, one=one):
                for u in range(unit):
                    one(lo + n * unit + u)
                return carry

            lax.fori_loop(0, whole // unit, body, 0)
            for c in range(lo + whole, hi):
                one(c)
            lo = hi

    for i, copy in enumerate(large):
        copy.wait()
        for col in range(4):

            @pl.when(me == col)
            def _(col=col, i=i):
                run(col, i)


def turn_amplitudes(a_ref, b_ref, c_ref, out_ref, rows_ref, turned_ref):
    _, slots, rows, occ = a_ref.shape
    total = a_ref[0] + b_ref[0] + c_ref[...]
    rows_ref[...] = total.astype(jnp.float32).reshape(slots * rows, occ)
    half = occ // 2
    to = lax.broadcasted_iota(jnp.int32, (occ, occ), 0)
    frm = lax.broadcasted_iota(jnp.int32, (occ, occ), 1)
    pick = (frm == 2 * (to % half) + to // half).astype(jnp.bfloat16)
    for a in range(rows):
        block = rows_ref[pl.ds(a, slots, stride=rows), :].astype(jnp.bfloat16)
        turned = lax.dot_general(pick, block, (((1,), (1,)), ((), ())), preferred_element_type=jnp.float32)
        turned_ref[pl.ds(a, half, stride=rows), :] = jnp.concatenate([turned[:half], turned[half:]], axis=1)
    shift = own_shift()
    for i, member in enumerate(SAME):
        for d, partner in enumerate(PARTNERS):
            row = (member ^ partner) ^ shift
            out_ref[i, d] = turned_ref[pl.ds(pl.multiple_of(row * rows, rows), rows), :].astype(jnp.bfloat16)


def fold_integrals(int_hbm, occ_hbm, vir_hbm, after_hbm, out_ref, lab_ref, vec_ref, int_ref, occ_ref, vir_ref, small, sems):
    _, v, width = int_ref.shape
    near = [pltpu.make_async_copy(vir_hbm, vir_ref, small.at[0]), pltpu.make_async_copy(occ_hbm, occ_ref, small.at[1])]
    step = v // sems.shape[1]
    copies = [
        [
            pltpu.make_async_copy(int_hbm.at[k, pl.ds(c, step)], int_ref.at[k, pl.ds(c, step)], sems.at[k, c // step])
            for c in range(0, v, step)
        ]
        for k in range(2)
    ]
    for copy in near + copies[0] + copies[1]:
        copy.start()
    for copy in near:
        copy.wait()
    begins = []
    for label in range(1, 8):
        lo, hi = jnp.int32(0), jnp.int32(v)
        for _ in range(v.bit_length()):
            mid = jnp.minimum((lo + hi) // 2, v - 1)
            reached = vir_ref[mid] >= label
            lo, hi = jnp.where(reached, lo, mid + 1), jnp.where(reached, mid, hi)
        begins.append(hi)

    def labels_of(orbital):
        return sum((orbital >= begin).astype(jnp.int32) for begin in begins)

    for c in range(0, v, 80):
        at = lax.broadcasted_iota(jnp.int32, (80, 128), 0) + c
        lab_ref[c : c + 80, :] = labels_of(at).astype(jnp.bfloat16)
    vir_vec = labels_of(lax.broadcasted_iota(jnp.int32, (1, width), 1))
    vec_ref[...] = vir_vec
    for k in range(2):
        label = occ_ref[lax.axis_index("row") * 2 + k] ^ occ_ref[1 + lax.axis_index("col")]
        b_labels = (vir_vec ^ label).astype(jnp.bfloat16)
        for i, copy in enumerate(copies[k]):
            copy.wait()
            for c in range(i * step, (i + 1) * step, 80):
                rows = slice(c, c + 80)
                c_labels = lab_ref[rows, :]
                for n in range(FOLD // 128):
                    total = None
                    for b in range(n * 128, width, FOLD):
                        size = min(128, width - b)
                        x = int_ref[k, rows, b : b + size]
                        x = jnp.where(c_labels[:, :size] == b_labels[:, b : b + size], x, jnp.zeros_like(x))
                        if size < 128:
                            x = jnp.concatenate([x, jnp.zeros((80, 128 - size), x.dtype)], axis=1)
                        total = x if total is None else total + x
                    out_ref[k, rows, n * 128 : (n + 1) * 128] = total
        out_ref[k, v:, :] = jnp.zeros((out_ref.shape[1] - v, FOLD), out_ref.dtype)


def contract(terms, last, *refs):
    quarters, partners = sorted({p for p, _ in terms}), sorted({d for _, d in terms})
    cut = len(quarters) + len(partners)
    t_refs, w_refs = refs[: len(quarters)], refs[len(quarters) : cut]
    lab_ref, vec_ref, occ_ref = refs[cut : cut + 3]
    sum_refs, (out_ref, a_lab_ref) = refs[cut + 3 : -2], refs[-2:]
    near, far, rows, lanes = t_refs[0].shape
    v = vec_ref.shape[1]
    me = lax.axis_index("col")
    own = lax.axis_index("row")
    shift = own_shift()
    for i, member in enumerate(SAME):
        label = lab_ref[pl.ds(pl.multiple_of((member ^ shift) * rows, rows), rows), :]
        a_lab_ref[i * rows : (i + 1) * rows, :] = label
    high = lax.broadcasted_iota(jnp.int32, (1, lanes), 1) >= QUARTER

    def labels_at(c):
        x = vec_ref[:, c : min(c + QUARTER, v)]
        if c + QUARTER > v:
            x = jnp.concatenate([x, jnp.full((1, c + QUARTER - v), 64, jnp.int32)], axis=1)
        return jnp.concatenate([x, x], axis=1)

    for col in range(4):

        @pl.when(me == col)
        def _(col=col):
            total = sum_refs[0][...] if sum_refs else None
            a_labels = a_lab_ref[...]
            blocks = [(p, d, c) for p, d in terms for c in range((col ^ p) * QUARTER, v, FOLD)]
            for n in range(0, len(blocks), GROUP):
                lhs, w = [], []
                for p, d, c in blocks[n : n + GROUP]:
                    other = 2 * (own ^ PARTNERS[d])
                    wanted = jnp.where(high, occ_ref[other + 1], occ_ref[other]) ^ occ_ref[0]
                    x = t_refs[quarters.index(p)][:, d].reshape(near * rows, lanes)
                    c_labels = (labels_at(c) ^ wanted).astype(jnp.bfloat16)
                    lhs.append(jnp.where(a_labels == c_labels, x, jnp.zeros_like(x)))
                    w += [w_refs[partners.index(d)][k, c : c + QUARTER, :] for k in range(2)]
                lhs = lhs[0] if len(lhs) == 1 else jnp.concatenate(lhs, axis=1)
                part = jnp.dot(lhs, jnp.concatenate(w, axis=0), preferred_element_type=jnp.float32)
                total = part if total is None else total + part
            out_ref[...] = total * SEND_SCALE if last else total


def prepare(res_ref, vir_vec_ref, energy_vec_ref, occ_ref, vir_ref, occ_e_ref, vir_e_ref, plain_ref, factor_ref):
    rows, v = res_ref.shape
    first_a = lax.axis_index("row") * rows
    j = 1 + lax.axis_index("col")
    row_id = lax.broadcasted_iota(jnp.int32, (rows, 128), 0)
    a_labels = jnp.zeros((rows, 128), jnp.int32)
    a_energy = jnp.zeros((rows, 128), jnp.float32)
    for a in range(rows):
        a_labels = jnp.where(row_id == a, vir_ref[first_a + a], a_labels)
        a_energy = jnp.where(row_id == a, vir_e_ref[first_a + a], a_energy)
    b_labels = vir_vec_ref[...] ^ occ_ref[0] ^ occ_ref[j]
    for b in range(0, v, 128):
        width = min(128, v - b)
        at = slice(b, b + width)
        denominator = occ_e_ref[0] - a_energy[:, :width] + (occ_e_ref[j] - energy_vec_ref[:, at])
        plain_ref[:, at] = res_ref[:, at] / denominator
        factor_ref[:, at] = jnp.where(a_labels[:, :width] == b_labels[:, at], (1.0 / SEND_SCALE) / denominator, 0.0)


def finish(part_ref, plain_ref, factor_ref, out_ref):
    total = part_ref[...]
    v = out_ref.shape[1]
    for b in range(0, v, FOLD):
        width = min(FOLD, v - b)
        at = slice(b, b + width)
        out_ref[:, at] = plain_ref[:, at] + factor_ref[:, at] * total[:, :width]


def local(
    amplitudes,
    integrals,
    occupied_irrep,
    virtual_irrep,
    occupied_energy,
    virtual_energy,
    residual_in,
):
    o_win, rows, cols = amplitudes.shape
    occ_local, v, n_local = integrals.shape
    n_row = o_win // occ_local
    near = n_row // FAR
    smem = pl.BlockSpec(memory_space=pltpu.SMEM)
    vmem = pl.BlockSpec(memory_space=pltpu.VMEM)
    hbm = pl.BlockSpec(memory_space=pltpu.HBM)
    big = pltpu.CompilerParams(vmem_limit_bytes=24 * 1024 * 1024)
    occ_vec = occupied_irrep.reshape(1, o_win)

    chunks = 6
    def folded(odd, after):
        return pl.pallas_call(
            functools.partial(fold_amplitudes, odd),
            out_shape=jax.ShapeDtypeStruct((2, QUARTER, rows, o_win), jnp.bfloat16),
            in_specs=[hbm] * 5,
            out_specs=vmem,
            scratch_shapes=[
                pltpu.VMEM((cols, rows, o_win), jnp.bfloat16),
                pltpu.VMEM((1, o_win), jnp.int32),
                pltpu.SMEM((o_win,), jnp.int32),
                pltpu.SMEM((v,), jnp.int32),
                pltpu.VMEM((8, rows, o_win), jnp.bfloat16),
                pltpu.SemaphoreType.DMA((3 + chunks,)),
            ],
            compiler_params=big,
            name="fold_amplitudes",
        )(
            pltpu.with_memory_space_constraint(amplitudes.transpose(2, 1, 0), pltpu.HBM),
            pltpu.with_memory_space_constraint(occ_vec, pltpu.HBM),
            pltpu.with_memory_space_constraint(occupied_irrep, pltpu.HBM),
            pltpu.with_memory_space_constraint(virtual_irrep, pltpu.HBM),
            after,
        )

    send = folded(1, pltpu.with_memory_space_constraint(occupied_irrep, pltpu.HBM))
    keep = folded(0, send)

    def swap(x, p):
        return lax.ppermute(x, "col", [(m, m ^ p) for m in range(4)])

    got = swap(send, 1)
    passed = keep[1] + got[1]
    w, labels, vir_vec = pl.pallas_call(
        fold_integrals,
        out_shape=[
            jax.ShapeDtypeStruct((occ_local, -(-v // QUARTER) * QUARTER, FOLD), jnp.bfloat16),
            jax.ShapeDtypeStruct((v, 128), jnp.bfloat16),
            jax.ShapeDtypeStruct((1, v), jnp.int32),
        ],
        in_specs=[hbm] * 4,
        out_specs=[vmem] * 3,
        scratch_shapes=[
            pltpu.VMEM((occ_local, v, n_local), jnp.bfloat16),
            pltpu.SMEM((o_win,), jnp.int32),
            pltpu.SMEM((v,), jnp.int32),
            pltpu.SemaphoreType.DMA((2,)),
            pltpu.SemaphoreType.DMA((occ_local, 5)),
        ],
        compiler_params=big,
        name="fold_integrals",
    )(
        pltpu.with_memory_space_constraint(integrals, pltpu.HBM),
        pltpu.with_memory_space_constraint(occupied_irrep, pltpu.HBM),
        pltpu.with_memory_space_constraint(virtual_irrep, pltpu.HBM),
        passed,
    )
    far = swap(passed, 2)
    turned = pl.pallas_call(
        turn_amplitudes,
        out_shape=jax.ShapeDtypeStruct((near, FAR, rows, occ_local * QUARTER), jnp.bfloat16),
        in_specs=[vmem] * 3,
        out_specs=vmem,
        scratch_shapes=[
            pltpu.VMEM((QUARTER * rows, o_win), jnp.float32),
            pltpu.VMEM((n_row * rows, o_win), jnp.float32),
        ],
        compiler_params=big,
        cost_estimate=pl.CostEstimate(flops=4 * 10**10, bytes_accessed=10**6, transcendentals=0),
        name="turn_amplitudes",
    )(keep, got, far)
    classes = [[member ^ partner for member in SAME] for partner in PARTNERS]
    mine = lax.all_to_all(turned, "row", split_axis=0, concat_axis=0, tiled=True, axis_index_groups=classes)
    across = swap(mine, 2)

    gathered = [w, lax.ppermute(w, "row", [(r, r ^ PARTNERS[1]) for r in range(n_row)])]
    quarters = [mine, swap(mine, 1), across, swap(across, 1)]

    def contracted(terms, last, sums):
        used = [quarters[p] for p in sorted({p for p, _ in terms})] + [gathered[d] for d in sorted({d for _, d in terms})]
        return pl.pallas_call(
            functools.partial(contract, terms, last),
            out_shape=jax.ShapeDtypeStruct((near * rows, FOLD), jnp.float32),
            in_specs=[vmem] * (len(used) + 2) + [smem] + [vmem] * len(sums),
            out_specs=vmem,
            scratch_shapes=[pltpu.VMEM((near * rows, occ_local * QUARTER), jnp.bfloat16)],
            compiler_params=big,
            name="contract",
        )(*used, labels, vir_vec, occupied_irrep, *sums)

    early = [(0, 0), (1, 0), (2, 0)]
    partial = contracted(early, False, [])
    partial = contracted([(0, 1), (1, 1), (2, 1), (3, 0), (3, 1)], True, [partial])
    parts = lax.all_to_all(
        partial.astype(SEND_TYPE).reshape(near, rows, FOLD),
        "row",
        split_axis=0,
        concat_axis=0,
        tiled=True,
        axis_index_groups=classes,
    )
    plain, factor = pl.pallas_call(
        prepare,
        out_shape=[jax.ShapeDtypeStruct(residual_in.shape, jnp.float32)] * 2,
        in_specs=[vmem] * 3 + [smem] * 4,
        out_specs=[vmem, vmem],
        compiler_params=big,
        name="prepare",
    )(
        residual_in,
        vir_vec,
        virtual_energy.reshape(1, v),
        occupied_irrep,
        virtual_irrep,
        occupied_energy,
        virtual_energy,
    )
    return pl.pallas_call(
        finish,
        out_shape=jax.ShapeDtypeStruct(residual_in.shape, jnp.float32),
        in_specs=[vmem] * 3,
        out_specs=vmem,
        compiler_params=big,
        name="finish",
    )(jnp.sum(parts.astype(jnp.float32), axis=0), plain, factor)


def solution(mesh):
    in_specs = (P(None, "row", "col"), P("row", None, "col"), P(), P(), P(), P(), P("row", "col"))
    out_specs = P("row", "col")
    return jax.shard_map(local, mesh=mesh, in_specs=in_specs, out_specs=out_specs, check_vma=False)
```

```python
import functools

import jax
import jax.numpy as jnp
from jax import lax
from jax.experimental import pallas as pl
from jax.experimental.pallas import tpu as pltpu
from jax.sharding import PartitionSpec as P

NJ = 4
FAR = 2
PARTNERS = (0, 48)
FOLD = 256
QUARTER = FOLD // 4
SEND_TYPE = jnp.float16
SEND_SCALE = 64.0


def colour(row):
    return (row >> 5) & 1


SAME = [row for row in range(64) if colour(row) == 0]


def own_shift():
    mine = colour(lax.axis_index("row"))
    shift = jnp.int32(0)
    for c in range(1, FAR):
        shift = jnp.where(mine == c, PARTNERS[c], shift)
    return shift


def fold_amplitudes(odd, amp_hbm, occ_vec_hbm, occ_hbm, vir_hbm, after_hbm, out_ref, amp_ref, occ_vec_ref, occ_ref, vir_ref, mask_ref, sems):
    cols, rows, occ = amp_ref.shape
    step = cols // (sems.shape[0] - 3)
    small = [
        pltpu.make_async_copy(vir_hbm, vir_ref, sems.at[0]),
        pltpu.make_async_copy(occ_hbm, occ_ref, sems.at[1]),
        pltpu.make_async_copy(occ_vec_hbm, occ_vec_ref, sems.at[2]),
    ]
    large = [
        pltpu.make_async_copy(amp_hbm.at[pl.ds(c, step)], amp_ref.at[pl.ds(c, step)], sems.at[3 + c // step])
        for c in range(0, cols, step)
    ]
    for copy in small + large:
        copy.start()
    for copy in small:
        copy.wait()
    me = lax.axis_index("col")
    first_a = lax.axis_index("row") * rows
    row_id = lax.broadcasted_iota(jnp.int32, (rows, occ), 0)
    a_labels = jnp.zeros((rows, occ), jnp.int32)
    for a in range(rows):
        a_labels = jnp.where(row_id == a, vir_ref[first_a + a], a_labels)
    wanted = occ_ref[0] ^ occ_vec_ref[...] ^ a_labels
    for label in range(8):
        mask_ref[label] = jnp.where(wanted == label, 1.0, 0.0).astype(jnp.bfloat16)
    def run(col, i):
        start = col * cols
        lo, end = i * step, (i + 1) * step
        while lo < end:
            slot = (start + lo) % FOLD
            hi = min(end, lo + QUARTER - slot % QUARTER, FOLD if lo < FOLD else end)
            p = (slot // QUARTER) ^ col
            first = slot % QUARTER
            again = lo >= FOLD
            if p % 2 != odd:
                lo = hi
                continue

            def one(c, lo=lo, p=p, first=first, again=again):
                x = amp_ref[c] * mask_ref[vir_ref[start + c]]
                place = c - lo + first
                if again:
                    x = x + out_ref[p // 2, place]
                out_ref[p // 2, place] = x

            unit = 10
            whole = (hi - lo) // unit * unit

            def body(n, carry, lo=lo, one=one):
                for u in range(unit):
                    one(lo + n * unit + u)
                return carry

            lax.fori_loop(0, whole // unit, body, 0)
            for c in range(lo + whole, hi):
                one(c)
            lo = hi

    for i, copy in enumerate(large):
        copy.wait()
        for col in range(4):

            @pl.when(me == col)
            def _(col=col, i=i):
                run(col, i)


def turn_amplitudes(a_ref, b_ref, c_ref, out_ref, rows_ref, turned_ref):
    _, slots, rows, occ = a_ref.shape
    total = a_ref[0] + b_ref[0] + c_ref[...]
    rows_ref[...] = total.astype(jnp.float32).reshape(slots * rows, occ)
    half = occ // 2
    to = lax.broadcasted_iota(jnp.int32, (occ, occ), 0)
    frm = lax.broadcasted_iota(jnp.int32, (occ, occ), 1)
    pick = (frm == 2 * (to % half) + to // half).astype(jnp.bfloat16)
    for a in range(rows):
        block = rows_ref[pl.ds(a, slots, stride=rows), :].astype(jnp.bfloat16)
        turned = lax.dot_general(pick, block, (((1,), (1,)), ((), ())), preferred_element_type=jnp.float32)
        turned_ref[pl.ds(a, half, stride=rows), :] = jnp.concatenate([turned[:half], turned[half:]], axis=1)
    shift = own_shift()
    for i, member in enumerate(SAME):
        for d, partner in enumerate(PARTNERS):
            row = (member ^ partner) ^ shift
            out_ref[i, d] = turned_ref[pl.ds(pl.multiple_of(row * rows, rows), rows), :].astype(jnp.bfloat16)


def fold_integrals(int_hbm, occ_hbm, vir_hbm, after_hbm, out_ref, lab_ref, vec_ref, tab_ref, int_ref, occ_ref, vir_ref, small, sems):
    _, v, width = int_ref.shape
    near = [pltpu.make_async_copy(vir_hbm, vir_ref, small.at[0]), pltpu.make_async_copy(occ_hbm, occ_ref, small.at[1])]
    step = v // sems.shape[1]
    copies = [
        [
            pltpu.make_async_copy(int_hbm.at[k, pl.ds(c, step)], int_ref.at[k, pl.ds(c, step)], sems.at[k, c // step])
            for c in range(0, v, step)
        ]
        for k in range(2)
    ]
    for copy in near + copies[0] + copies[1]:
        copy.start()
    for copy in near:
        copy.wait()
    begins = []
    for label in range(1, 8):
        lo, hi = jnp.int32(0), jnp.int32(v)
        for _ in range(v.bit_length()):
            mid = jnp.minimum((lo + hi) // 2, v - 1)
            reached = vir_ref[mid] >= label
            lo, hi = jnp.where(reached, lo, mid + 1), jnp.where(reached, mid, hi)
        begins.append(hi)

    def labels_of(orbital):
        return sum((orbital >= begin).astype(jnp.int32) for begin in begins)

    for c in range(0, v, 80):
        at = lax.broadcasted_iota(jnp.int32, (80, 128), 0) + c
        lab_ref[c : c + 80, :] = labels_of(at).astype(jnp.bfloat16)
    vir_vec = labels_of(lax.broadcasted_iota(jnp.int32, (1, width), 1))
    vec_ref[...] = vir_vec
    for block in range(tab_ref.shape[0]):
        size = min(QUARTER, v - block * QUARTER)
        x = jnp.full((1, QUARTER), 64, jnp.int32)
        if size > 0:
            x = vir_vec[:, block * QUARTER : block * QUARTER + size]
            if size < QUARTER:
                x = jnp.concatenate([x, jnp.full((1, QUARTER - size), 64, jnp.int32)], axis=1)
        tab_ref[block : block + 1, :] = jnp.concatenate([x, x], axis=1)
    for k in range(2):
        label = occ_ref[lax.axis_index("row") * 2 + k] ^ occ_ref[1 + lax.axis_index("col")]
        b_labels = (vir_vec ^ label).astype(jnp.bfloat16)
        for i, copy in enumerate(copies[k]):
            copy.wait()
            for c in range(i * step, (i + 1) * step, 80):
                rows = slice(c, c + 80)
                c_labels = lab_ref[rows, :]
                for n in range(FOLD // 128):
                    total = None
                    for b in range(n * 128, width, FOLD):
                        size = min(128, width - b)
                        x = int_ref[k, rows, b : b + size]
                        x = jnp.where(c_labels[:, :size] == b_labels[:, b : b + size], x, jnp.zeros_like(x))
                        if size < 128:
                            x = jnp.concatenate([x, jnp.zeros((80, 128 - size), x.dtype)], axis=1)
                        total = x if total is None else total + x
                    out_ref[k, rows, n * 128 : (n + 1) * 128] = total
        out_ref[k, v:, :] = jnp.zeros((out_ref.shape[1] - v, FOLD), out_ref.dtype)


def contract(terms, last, *refs):
    quarters, partners = sorted({p for p, _ in terms}), sorted({d for _, d in terms})
    cut = len(quarters) + len(partners)
    t_refs, w_refs = refs[: len(quarters)], refs[len(quarters) : cut]
    lab_ref, tab_ref, occ_ref = refs[cut : cut + 3]
    sum_refs, (out_ref, a_lab_ref) = refs[cut + 3 : -2], refs[-2:]
    near, far, rows, lanes = t_refs[0].shape
    tall = w_refs[0].shape[1]
    me = lax.axis_index("col")
    own = lax.axis_index("row")
    shift = own_shift()
    for i, member in enumerate(SAME):
        label = lab_ref[pl.ds(pl.multiple_of((member ^ shift) * rows, rows), rows), :]
        a_lab_ref[i * rows : (i + 1) * rows, :] = label
    high = lax.broadcasted_iota(jnp.int32, (1, lanes), 1) >= QUARTER
    a_labels = a_lab_ref[...]
    total = sum_refs[0][...] if sum_refs else None
    blocks = [(p, d, t) for p, d in terms for t in range(tab_ref.shape[0] // 4)]
    for n in range(0, len(blocks), 2):
        lhs, w = [], []
        for p, d, t in blocks[n : n + 2]:
            other = 2 * (own ^ PARTNERS[d])
            wanted = jnp.where(high, occ_ref[other + 1], occ_ref[other]) ^ occ_ref[0]
            block = 4 * t + (me ^ p)
            x = t_refs[quarters.index(p)][:, d].reshape(near * rows, lanes)
            c_labels = (tab_ref[pl.ds(block, 1), :] ^ wanted).astype(jnp.bfloat16)
            lhs.append(jnp.where(a_labels == c_labels, x, jnp.zeros_like(x)))
            c = pl.multiple_of(jnp.minimum(block * QUARTER, tall - QUARTER), QUARTER)
            w += [w_refs[partners.index(d)][k, pl.ds(c, QUARTER), :] for k in range(2)]
        lhs = lhs[0] if len(lhs) == 1 else jnp.concatenate(lhs, axis=1)
        part = jnp.dot(lhs, jnp.concatenate(w, axis=0), preferred_element_type=jnp.float32)
        total = part if total is None else total + part
    out_ref[...] = total * SEND_SCALE if last else total


def prepare(res_ref, vir_vec_ref, energy_vec_ref, occ_ref, vir_ref, occ_e_ref, vir_e_ref, plain_ref, factor_ref):
    rows, v = res_ref.shape
    first_a = lax.axis_index("row") * rows
    j = 1 + lax.axis_index("col")
    row_id = lax.broadcasted_iota(jnp.int32, (rows, 128), 0)
    a_labels = jnp.zeros((rows, 128), jnp.int32)
    a_energy = jnp.zeros((rows, 128), jnp.float32)
    for a in range(rows):
        a_labels = jnp.where(row_id == a, vir_ref[first_a + a], a_labels)
        a_energy = jnp.where(row_id == a, vir_e_ref[first_a + a], a_energy)
    b_labels = vir_vec_ref[...] ^ occ_ref[0] ^ occ_ref[j]
    for b in range(0, v, 128):
        width = min(128, v - b)
        at = slice(b, b + width)
        denominator = occ_e_ref[0] - a_energy[:, :width] + (occ_e_ref[j] - energy_vec_ref[:, at])
        plain_ref[:, at] = res_ref[:, at] / denominator
        factor_ref[:, at] = jnp.where(a_labels[:, :width] == b_labels[:, at], (1.0 / SEND_SCALE) / denominator, 0.0)


def finish(part_ref, plain_ref, factor_ref, out_ref):
    total = part_ref[...]
    v = out_ref.shape[1]
    for b in range(0, v, FOLD):
        width = min(FOLD, v - b)
        at = slice(b, b + width)
        out_ref[:, at] = plain_ref[:, at] + factor_ref[:, at] * total[:, :width]


def local(
    amplitudes,
    integrals,
    occupied_irrep,
    virtual_irrep,
    occupied_energy,
    virtual_energy,
    residual_in,
):
    o_win, rows, cols = amplitudes.shape
    occ_local, v, n_local = integrals.shape
    n_row = o_win // occ_local
    near = n_row // FAR
    smem = pl.BlockSpec(memory_space=pltpu.SMEM)
    vmem = pl.BlockSpec(memory_space=pltpu.VMEM)
    hbm = pl.BlockSpec(memory_space=pltpu.HBM)
    big = pltpu.CompilerParams(vmem_limit_bytes=24 * 1024 * 1024)
    occ_vec = occupied_irrep.reshape(1, o_win)

    chunks = 6
    def folded(odd, after):
        return pl.pallas_call(
            functools.partial(fold_amplitudes, odd),
            out_shape=jax.ShapeDtypeStruct((2, QUARTER, rows, o_win), jnp.bfloat16),
            in_specs=[hbm] * 5,
            out_specs=vmem,
            scratch_shapes=[
                pltpu.VMEM((cols, rows, o_win), jnp.bfloat16),
                pltpu.VMEM((1, o_win), jnp.int32),
                pltpu.SMEM((o_win,), jnp.int32),
                pltpu.SMEM((v,), jnp.int32),
                pltpu.VMEM((8, rows, o_win), jnp.bfloat16),
                pltpu.SemaphoreType.DMA((3 + chunks,)),
            ],
            compiler_params=big,
            name="fold_amplitudes",
        )(
            pltpu.with_memory_space_constraint(amplitudes.transpose(2, 1, 0), pltpu.HBM),
            pltpu.with_memory_space_constraint(occ_vec, pltpu.HBM),
            pltpu.with_memory_space_constraint(occupied_irrep, pltpu.HBM),
            pltpu.with_memory_space_constraint(virtual_irrep, pltpu.HBM),
            after,
        )

    send = folded(1, pltpu.with_memory_space_constraint(occupied_irrep, pltpu.HBM))
    keep = folded(0, send)

    def swap(x, p):
        return lax.ppermute(x, "col", [(m, m ^ p) for m in range(4)])

    got = swap(send, 1)
    passed = keep[1] + got[1]
    w, labels, vir_vec, table = pl.pallas_call(
        fold_integrals,
        out_shape=[
            jax.ShapeDtypeStruct((occ_local, -(-v // QUARTER) * QUARTER, FOLD), jnp.bfloat16),
            jax.ShapeDtypeStruct((v, 128), jnp.bfloat16),
            jax.ShapeDtypeStruct((1, v), jnp.int32),
            jax.ShapeDtypeStruct((4 * (-(-v // FOLD)), 2 * QUARTER), jnp.int32),
        ],
        in_specs=[hbm] * 4,
        out_specs=[vmem] * 4,
        scratch_shapes=[
            pltpu.VMEM((occ_local, v, n_local), jnp.bfloat16),
            pltpu.SMEM((o_win,), jnp.int32),
            pltpu.SMEM((v,), jnp.int32),
            pltpu.SemaphoreType.DMA((2,)),
            pltpu.SemaphoreType.DMA((occ_local, 5)),
        ],
        compiler_params=big,
        name="fold_integrals",
    )(
        pltpu.with_memory_space_constraint(integrals, pltpu.HBM),
        pltpu.with_memory_space_constraint(occupied_irrep, pltpu.HBM),
        pltpu.with_memory_space_constraint(virtual_irrep, pltpu.HBM),
        passed,
    )
    far = swap(passed, 2)
    turned = pl.pallas_call(
        turn_amplitudes,
        out_shape=jax.ShapeDtypeStruct((near, FAR, rows, occ_local * QUARTER), jnp.bfloat16),
        in_specs=[vmem] * 3,
        out_specs=vmem,
        scratch_shapes=[
            pltpu.VMEM((QUARTER * rows, o_win), jnp.float32),
            pltpu.VMEM((n_row * rows, o_win), jnp.float32),
        ],
        compiler_params=big,
        cost_estimate=pl.CostEstimate(flops=4 * 10**10, bytes_accessed=10**6, transcendentals=0),
        name="turn_amplitudes",
    )(keep, got, far)
    classes = [[member ^ partner for member in SAME] for partner in PARTNERS]
    mine = lax.all_to_all(turned, "row", split_axis=0, concat_axis=0, tiled=True, axis_index_groups=classes)
    across = swap(mine, 2)

    gathered = [w, lax.ppermute(w, "row", [(r, r ^ PARTNERS[1]) for r in range(n_row)])]
    quarters = [mine, swap(mine, 1)]

    def contracted(terms, last, sums):
        used = [quarters[p] for p in sorted({p for p, _ in terms})] + [gathered[d] for d in sorted({d for _, d in terms})]
        return pl.pallas_call(
            functools.partial(contract, terms, last),
            out_shape=jax.ShapeDtypeStruct((near * rows, FOLD), jnp.float32),
            in_specs=[vmem] * (len(used) + 2) + [smem] + [vmem] * len(sums),
            out_specs=vmem,
            scratch_shapes=[pltpu.VMEM((near * rows, occ_local * QUARTER), jnp.bfloat16)],
            compiler_params=big,
            name="contract",
        )(*used, labels, table, occupied_irrep, *sums)

    partial = contracted([(0, 0)], False, [])
    across, partial = lax.optimization_barrier((across, partial))
    quarters += [across, swap(across, 1)]
    partial = contracted([(1, 0), (2, 0)], False, [partial])
    partial = contracted([(0, 1), (1, 1), (2, 1), (3, 0), (3, 1)], True, [partial])
    parts = lax.all_to_all(
        partial.astype(SEND_TYPE).reshape(near, rows, FOLD),
        "row",
        split_axis=0,
        concat_axis=0,
        tiled=True,
        axis_index_groups=classes,
    )
    plain, factor = pl.pallas_call(
        prepare,
        out_shape=[jax.ShapeDtypeStruct(residual_in.shape, jnp.float32)] * 2,
        in_specs=[vmem] * 3 + [smem] * 4,
        out_specs=[vmem, vmem],
        compiler_params=big,
        name="prepare",
    )(
        residual_in,
        vir_vec,
        virtual_energy.reshape(1, v),
        occupied_irrep,
        virtual_irrep,
        occupied_energy,
        virtual_energy,
    )
    return pl.pallas_call(
        finish,
        out_shape=jax.ShapeDtypeStruct(residual_in.shape, jnp.float32),
        in_specs=[vmem] * 3,
        out_specs=vmem,
        compiler_params=big,
        name="finish",
    )(jnp.sum(parts.astype(jnp.float32), axis=0), plain, factor)


def solution(mesh):
    in_specs = (P(None, "row", "col"), P("row", None, "col"), P(), P(), P(), P(), P("row", "col"))
    out_specs = P("row", "col")
    return jax.shard_map(local, mesh=mesh, in_specs=in_specs, out_specs=out_specs, check_vma=False)
```

```python
import functools

import jax
import jax.numpy as jnp
from jax import lax
from jax.experimental import pallas as pl
from jax.experimental.pallas import tpu as pltpu
from jax.sharding import PartitionSpec as P

NJ = 4
FAR = 2
PARTNERS = (0, 48)
FOLD = 256
QUARTER = FOLD // 4
SEND_TYPE = jnp.float16
SEND_SCALE = 64.0


def colour(row):
    return (row >> 5) & 1


SAME = [row for row in range(64) if colour(row) == 0]


def own_shift():
    mine = colour(lax.axis_index("row"))
    shift = jnp.int32(0)
    for c in range(1, FAR):
        shift = jnp.where(mine == c, PARTNERS[c], shift)
    return shift


def fold_amplitudes(odd, amp_hbm, occ_vec_hbm, occ_hbm, vir_hbm, after_hbm, out_ref, amp_ref, occ_vec_ref, occ_ref, vir_ref, mask_ref, sems):
    cols, rows, occ = amp_ref.shape
    step = cols // (sems.shape[0] - 3)
    small = [
        pltpu.make_async_copy(vir_hbm, vir_ref, sems.at[0]),
        pltpu.make_async_copy(occ_hbm, occ_ref, sems.at[1]),
        pltpu.make_async_copy(occ_vec_hbm, occ_vec_ref, sems.at[2]),
    ]
    large = [
        pltpu.make_async_copy(amp_hbm.at[pl.ds(c, step)], amp_ref.at[pl.ds(c, step)], sems.at[3 + c // step])
        for c in range(0, cols, step)
    ]
    for copy in small + large:
        copy.start()
    for copy in small:
        copy.wait()
    me = lax.axis_index("col")
    first_a = lax.axis_index("row") * rows
    row_id = lax.broadcasted_iota(jnp.int32, (rows, occ), 0)
    a_labels = jnp.zeros((rows, occ), jnp.int32)
    for a in range(rows):
        a_labels = jnp.where(row_id == a, vir_ref[first_a + a], a_labels)
    wanted = occ_ref[0] ^ occ_vec_ref[...] ^ a_labels
    for label in range(8):
        mask_ref[label] = jnp.where(wanted == label, 1.0, 0.0).astype(jnp.bfloat16)
    def run(col, i):
        start = col * cols
        lo, end = i * step, (i + 1) * step
        while lo < end:
            slot = (start + lo) % FOLD
            hi = min(end, lo + QUARTER - slot % QUARTER, FOLD if lo < FOLD else end)
            p = (slot // QUARTER) ^ col
            first = slot % QUARTER
            again = lo >= FOLD
            if p % 2 != odd:
                lo = hi
                continue

            def one(c, lo=lo, p=p, first=first, again=again):
                x = amp_ref[c] * mask_ref[vir_ref[start + c]]
                place = c - lo + first
                if again:
                    x = x + out_ref[p // 2, place]
                out_ref[p // 2, place] = x

            unit = 10
            whole = (hi - lo) // unit * unit

            def body(n, carry, lo=lo, one=one):
                for u in range(unit):
                    one(lo + n * unit + u)
                return carry

            lax.fori_loop(0, whole // unit, body, 0)
            for c in range(lo + whole, hi):
                one(c)
            lo = hi

    for i, copy in enumerate(large):
        copy.wait()
        for col in range(4):

            @pl.when(me == col)
            def _(col=col, i=i):
                run(col, i)


def turn_amplitudes(a_ref, b_ref, c_ref, out_ref, rows_ref, turned_ref):
    _, slots, rows, occ = a_ref.shape
    total = a_ref[0] + b_ref[0] + c_ref[...]
    rows_ref[...] = total.astype(jnp.float32).reshape(slots * rows, occ)
    half = occ // 2
    to = lax.broadcasted_iota(jnp.int32, (occ, occ), 0)
    frm = lax.broadcasted_iota(jnp.int32, (occ, occ), 1)
    pick = (frm == 2 * (to % half) + to // half).astype(jnp.bfloat16)
    for a in range(rows):
        block = rows_ref[pl.ds(a, slots, stride=rows), :].astype(jnp.bfloat16)
        turned = lax.dot_general(pick, block, (((1,), (1,)), ((), ())), preferred_element_type=jnp.float32)
        turned_ref[pl.ds(a, half, stride=rows), :] = jnp.concatenate([turned[:half], turned[half:]], axis=1)
    shift = own_shift()
    for i, member in enumerate(SAME):
        for d, partner in enumerate(PARTNERS):
            row = (member ^ partner) ^ shift
            out_ref[i, d] = turned_ref[pl.ds(pl.multiple_of(row * rows, rows), rows), :].astype(jnp.bfloat16)


def fold_integrals(int_hbm, occ_hbm, vir_hbm, after_hbm, out_ref, lab_ref, vec_ref, tab_ref, int_ref, occ_ref, vir_ref, small, sems):
    _, v, width = int_ref.shape
    near = [pltpu.make_async_copy(vir_hbm, vir_ref, small.at[0]), pltpu.make_async_copy(occ_hbm, occ_ref, small.at[1])]
    step = v // sems.shape[1]
    copies = [
        [
            pltpu.make_async_copy(int_hbm.at[k, pl.ds(c, step)], int_ref.at[k, pl.ds(c, step)], sems.at[k, c // step])
            for c in range(0, v, step)
        ]
        for k in range(2)
    ]
    for copy in near + copies[0] + copies[1]:
        copy.start()
    for copy in near:
        copy.wait()
    begins = []
    for label in range(1, 8):
        lo, hi = jnp.int32(0), jnp.int32(v)
        for _ in range(v.bit_length()):
            mid = jnp.minimum((lo + hi) // 2, v - 1)
            reached = vir_ref[mid] >= label
            lo, hi = jnp.where(reached, lo, mid + 1), jnp.where(reached, mid, hi)
        begins.append(hi)

    def labels_of(orbital):
        return sum((orbital >= begin).astype(jnp.int32) for begin in begins)

    for c in range(0, v, 80):
        at = lax.broadcasted_iota(jnp.int32, (80, 128), 0) + c
        lab_ref[c : c + 80, :] = labels_of(at).astype(jnp.bfloat16)
    vir_vec = labels_of(lax.broadcasted_iota(jnp.int32, (1, width), 1))
    vec_ref[...] = vir_vec
    high = lax.broadcasted_iota(jnp.int32, (1, 2 * QUARTER), 1) >= QUARTER
    wanted = []
    for partner in PARTNERS:
        other = 2 * (lax.axis_index("row") ^ partner)
        wanted.append(jnp.where(high, occ_ref[other + 1], occ_ref[other]) ^ occ_ref[0])
    for block in range(tab_ref.shape[1]):
        size = min(QUARTER, v - block * QUARTER)
        x = jnp.full((1, QUARTER), 64, jnp.int32)
        if size > 0:
            x = vir_vec[:, block * QUARTER : block * QUARTER + size]
            if size < QUARTER:
                x = jnp.concatenate([x, jnp.full((1, QUARTER - size), 64, jnp.int32)], axis=1)
        for d in range(FAR):
            tab_ref[d, block : block + 1, :] = jnp.concatenate([x, x], axis=1) ^ wanted[d]
    for k in range(2):
        label = occ_ref[lax.axis_index("row") * 2 + k] ^ occ_ref[1 + lax.axis_index("col")]
        b_labels = (vir_vec ^ label).astype(jnp.bfloat16)
        for i, copy in enumerate(copies[k]):
            copy.wait()
            for c in range(i * step, (i + 1) * step, 80):
                rows = slice(c, c + 80)
                c_labels = lab_ref[rows, :]
                for n in range(FOLD // 128):
                    total = None
                    for b in range(n * 128, width, FOLD):
                        size = min(128, width - b)
                        x = int_ref[k, rows, b : b + size]
                        x = jnp.where(c_labels[:, :size] == b_labels[:, b : b + size], x, jnp.zeros_like(x))
                        if size < 128:
                            x = jnp.concatenate([x, jnp.zeros((80, 128 - size), x.dtype)], axis=1)
                        total = x if total is None else total + x
                    out_ref[k, rows, n * 128 : (n + 1) * 128] = total
        out_ref[k, v:, :] = jnp.zeros((out_ref.shape[1] - v, FOLD), out_ref.dtype)


def contract(terms, last, *refs):
    quarters, partners = sorted({p for p, _ in terms}), sorted({d for _, d in terms})
    cut = len(quarters) + len(partners)
    t_refs, w_refs = refs[: len(quarters)], refs[len(quarters) : cut]
    lab_ref, tab_ref = refs[cut : cut + 2]
    sum_refs, (out_ref, a_lab_ref) = refs[cut + 2 : -2], refs[-2:]
    near, far, rows, lanes = t_refs[0].shape
    tall = w_refs[0].shape[1]
    me = lax.axis_index("col")
    shift = own_shift()
    for i, member in enumerate(SAME):
        label = lab_ref[pl.ds(pl.multiple_of((member ^ shift) * rows, rows), rows), :]
        a_lab_ref[i * rows : (i + 1) * rows, :] = label
    a_labels = a_lab_ref[...]
    total = sum_refs[0][...] if sum_refs else None
    blocks = [(p, d, t) for p, d in terms for t in range(tab_ref.shape[1] // 4)]
    for n in range(0, len(blocks), 2):
        lhs, w = [], []
        for p, d, t in blocks[n : n + 2]:
            block = 4 * t + (me ^ p)
            x = t_refs[quarters.index(p)][:, d].reshape(near * rows, lanes)
            c_labels = tab_ref[d, pl.ds(block, 1), :].astype(jnp.bfloat16)
            lhs.append(jnp.where(a_labels == c_labels, x, jnp.zeros_like(x)))
            c = pl.multiple_of(jnp.minimum(block * QUARTER, tall - QUARTER), QUARTER)
            w += [w_refs[partners.index(d)][k, pl.ds(c, QUARTER), :] for k in range(2)]
        lhs = lhs[0] if len(lhs) == 1 else jnp.concatenate(lhs, axis=1)
        part = jnp.dot(lhs, jnp.concatenate(w, axis=0), preferred_element_type=jnp.float32)
        total = part if total is None else total + part
    out_ref[...] = total * SEND_SCALE if last else total


def prepare(res_ref, vir_vec_ref, energy_vec_ref, occ_ref, vir_ref, occ_e_ref, vir_e_ref, plain_ref, factor_ref):
    rows, v = res_ref.shape
    first_a = lax.axis_index("row") * rows
    j = 1 + lax.axis_index("col")
    row_id = lax.broadcasted_iota(jnp.int32, (rows, 128), 0)
    a_labels = jnp.zeros((rows, 128), jnp.int32)
    a_energy = jnp.zeros((rows, 128), jnp.float32)
    for a in range(rows):
        a_labels = jnp.where(row_id == a, vir_ref[first_a + a], a_labels)
        a_energy = jnp.where(row_id == a, vir_e_ref[first_a + a], a_energy)
    b_labels = vir_vec_ref[...] ^ occ_ref[0] ^ occ_ref[j]
    for b in range(0, v, 128):
        width = min(128, v - b)
        at = slice(b, b + width)
        denominator = occ_e_ref[0] - a_energy[:, :width] + (occ_e_ref[j] - energy_vec_ref[:, at])
        plain_ref[:, at] = res_ref[:, at] / denominator
        factor_ref[:, at] = jnp.where(a_labels[:, :width] == b_labels[:, at], (1.0 / SEND_SCALE) / denominator, 0.0)


def finish(part_ref, plain_ref, factor_ref, out_ref):
    total = part_ref[...]
    v = out_ref.shape[1]
    for b in range(0, v, FOLD):
        width = min(FOLD, v - b)
        at = slice(b, b + width)
        out_ref[:, at] = plain_ref[:, at] + factor_ref[:, at] * total[:, :width]


def local(
    amplitudes,
    integrals,
    occupied_irrep,
    virtual_irrep,
    occupied_energy,
    virtual_energy,
    residual_in,
):
    o_win, rows, cols = amplitudes.shape
    occ_local, v, n_local = integrals.shape
    n_row = o_win // occ_local
    near = n_row // FAR
    smem = pl.BlockSpec(memory_space=pltpu.SMEM)
    vmem = pl.BlockSpec(memory_space=pltpu.VMEM)
    hbm = pl.BlockSpec(memory_space=pltpu.HBM)
    big = pltpu.CompilerParams(vmem_limit_bytes=24 * 1024 * 1024)
    occ_vec = occupied_irrep.reshape(1, o_win)

    chunks = 6
    def folded(odd, after):
        return pl.pallas_call(
            functools.partial(fold_amplitudes, odd),
            out_shape=jax.ShapeDtypeStruct((2, QUARTER, rows, o_win), jnp.bfloat16),
            in_specs=[hbm] * 5,
            out_specs=vmem,
            scratch_shapes=[
                pltpu.VMEM((cols, rows, o_win), jnp.bfloat16),
                pltpu.VMEM((1, o_win), jnp.int32),
                pltpu.SMEM((o_win,), jnp.int32),
                pltpu.SMEM((v,), jnp.int32),
                pltpu.VMEM((8, rows, o_win), jnp.bfloat16),
                pltpu.SemaphoreType.DMA((3 + chunks,)),
            ],
            compiler_params=big,
            name="fold_amplitudes",
        )(
            pltpu.with_memory_space_constraint(amplitudes.transpose(2, 1, 0), pltpu.HBM),
            pltpu.with_memory_space_constraint(occ_vec, pltpu.HBM),
            pltpu.with_memory_space_constraint(occupied_irrep, pltpu.HBM),
            pltpu.with_memory_space_constraint(virtual_irrep, pltpu.HBM),
            after,
        )

    send = folded(1, pltpu.with_memory_space_constraint(occupied_irrep, pltpu.HBM))
    keep = folded(0, send)

    def swap(x, p):
        return lax.ppermute(x, "col", [(m, m ^ p) for m in range(4)])

    got = swap(send, 1)
    passed = keep[1] + got[1]
    w, labels, vir_vec, table = pl.pallas_call(
        fold_integrals,
        out_shape=[
            jax.ShapeDtypeStruct((occ_local, -(-v // QUARTER) * QUARTER, FOLD), jnp.bfloat16),
            jax.ShapeDtypeStruct((v, 128), jnp.bfloat16),
            jax.ShapeDtypeStruct((1, v), jnp.int32),
            jax.ShapeDtypeStruct((FAR, 4 * (-(-v // FOLD)), 2 * QUARTER), jnp.int32),
        ],
        in_specs=[hbm] * 4,
        out_specs=[vmem] * 4,
        scratch_shapes=[
            pltpu.VMEM((occ_local, v, n_local), jnp.bfloat16),
            pltpu.SMEM((o_win,), jnp.int32),
            pltpu.SMEM((v,), jnp.int32),
            pltpu.SemaphoreType.DMA((2,)),
            pltpu.SemaphoreType.DMA((occ_local, 5)),
        ],
        compiler_params=big,
        name="fold_integrals",
    )(
        pltpu.with_memory_space_constraint(integrals, pltpu.HBM),
        pltpu.with_memory_space_constraint(occupied_irrep, pltpu.HBM),
        pltpu.with_memory_space_constraint(virtual_irrep, pltpu.HBM),
        passed,
    )
    far = swap(passed, 2)
    turned = pl.pallas_call(
        turn_amplitudes,
        out_shape=jax.ShapeDtypeStruct((near, FAR, rows, occ_local * QUARTER), jnp.bfloat16),
        in_specs=[vmem] * 3,
        out_specs=vmem,
        scratch_shapes=[
            pltpu.VMEM((QUARTER * rows, o_win), jnp.float32),
            pltpu.VMEM((n_row * rows, o_win), jnp.float32),
        ],
        compiler_params=big,
        cost_estimate=pl.CostEstimate(flops=4 * 10**10, bytes_accessed=10**6, transcendentals=0),
        name="turn_amplitudes",
    )(keep, got, far)
    classes = [[member ^ partner for member in SAME] for partner in PARTNERS]
    mine = lax.all_to_all(turned, "row", split_axis=0, concat_axis=0, tiled=True, axis_index_groups=classes)
    across = swap(mine, 2)

    gathered = [w, lax.ppermute(w, "row", [(r, r ^ PARTNERS[1]) for r in range(n_row)])]
    quarters = [mine, swap(mine, 1)]

    def contracted(terms, last, sums):
        used = [quarters[p] for p in sorted({p for p, _ in terms})] + [gathered[d] for d in sorted({d for _, d in terms})]
        return pl.pallas_call(
            functools.partial(contract, terms, last),
            out_shape=jax.ShapeDtypeStruct((near * rows, FOLD), jnp.float32),
            in_specs=[vmem] * (len(used) + 2 + len(sums)),
            out_specs=vmem,
            scratch_shapes=[pltpu.VMEM((near * rows, occ_local * QUARTER), jnp.bfloat16)],
            compiler_params=big,
            name="contract",
        )(*used, labels, table, *sums)

    partial = contracted([(0, 0)], False, [])
    across, partial = lax.optimization_barrier((across, partial))
    quarters += [across, swap(across, 1)]
    partial = contracted([(1, 0), (2, 0)], False, [partial])
    partial = contracted([(0, 1), (1, 1), (2, 1), (3, 0), (3, 1)], True, [partial])
    parts = lax.all_to_all(
        partial.astype(SEND_TYPE).reshape(near, rows, FOLD),
        "row",
        split_axis=0,
        concat_axis=0,
        tiled=True,
        axis_index_groups=classes,
    )
    plain, factor = pl.pallas_call(
        prepare,
        out_shape=[jax.ShapeDtypeStruct(residual_in.shape, jnp.float32)] * 2,
        in_specs=[vmem] * 3 + [smem] * 4,
        out_specs=[vmem, vmem],
        compiler_params=big,
        name="prepare",
    )(
        residual_in,
        vir_vec,
        virtual_energy.reshape(1, v),
        occupied_irrep,
        virtual_irrep,
        occupied_energy,
        virtual_energy,
    )
    return pl.pallas_call(
        finish,
        out_shape=jax.ShapeDtypeStruct(residual_in.shape, jnp.float32),
        in_specs=[vmem] * 3,
        out_specs=vmem,
        compiler_params=big,
        name="finish",
    )(jnp.sum(parts.astype(jnp.float32), axis=0), plain, factor)


def solution(mesh):
    in_specs = (P(None, "row", "col"), P("row", None, "col"), P(), P(), P(), P(), P("row", "col"))
    out_specs = P("row", "col")
    return jax.shard_map(local, mesh=mesh, in_specs=in_specs, out_specs=out_specs, check_vma=False)
```

```python
import functools

import jax
import jax.numpy as jnp
from jax import lax
from jax.experimental import pallas as pl
from jax.experimental.pallas import tpu as pltpu
from jax.sharding import PartitionSpec as P

NJ = 4
FAR = 2
PARTNERS = (0, 48)
FOLD = 256
QUARTER = FOLD // 4
SEND_TYPE = jnp.float16
SEND_SCALE = 64.0


def colour(row):
    return (row >> 5) & 1


SAME = [row for row in range(64) if colour(row) == 0]


def own_shift():
    mine = colour(lax.axis_index("row"))
    shift = jnp.int32(0)
    for c in range(1, FAR):
        shift = jnp.where(mine == c, PARTNERS[c], shift)
    return shift


def label_tables(occ_ref, vir_ref, lab_ref, vec_ref, tab_ref):
    v = vir_ref.shape[0]
    begins = []
    for label in range(1, 8):
        lo, hi = jnp.int32(0), jnp.int32(v)
        for _ in range(v.bit_length()):
            mid = jnp.minimum((lo + hi) // 2, v - 1)
            reached = vir_ref[mid] >= label
            lo, hi = jnp.where(reached, lo, mid + 1), jnp.where(reached, mid, hi)
        begins.append(hi)

    def labels_of(orbital):
        return sum((orbital >= begin).astype(jnp.int32) for begin in begins)

    for c in range(0, v, 80):
        at = lax.broadcasted_iota(jnp.int32, (80, 128), 0) + c
        lab_ref[c : c + 80, :] = labels_of(at).astype(jnp.bfloat16)
    vir_vec = labels_of(lax.broadcasted_iota(jnp.int32, (1, v), 1))
    row = lax.axis_index("row")
    for k in range(2):
        vec_ref[k] = vir_vec ^ (occ_ref[2 * row + k] ^ occ_ref[1 + lax.axis_index("col")])
    high = lax.broadcasted_iota(jnp.int32, (1, 2 * QUARTER), 1) >= QUARTER
    wanted = []
    for partner in PARTNERS:
        other = 2 * (row ^ partner)
        wanted.append(jnp.where(high, occ_ref[other + 1], occ_ref[other]) ^ occ_ref[0])
    for block in range(tab_ref.shape[1]):
        size = min(QUARTER, v - block * QUARTER)
        x = jnp.full((1, QUARTER), 64, jnp.int32)
        if size > 0:
            x = vir_vec[:, block * QUARTER : block * QUARTER + size]
            if size < QUARTER:
                x = jnp.concatenate([x, jnp.full((1, QUARTER - size), 64, jnp.int32)], axis=1)
        for d in range(FAR):
            tab_ref[d, block : block + 1, :] = jnp.concatenate([x, x], axis=1) ^ wanted[d]


def fold_amplitudes(odd, amp_hbm, occ_vec_hbm, occ_hbm, vir_hbm, after_hbm, out_ref, *refs):
    tables, (amp_ref, occ_vec_ref, occ_ref, vir_ref, mask_ref, sems) = refs[:-6], refs[-6:]
    cols, rows, occ = amp_ref.shape
    step = cols // (sems.shape[0] - 3)
    small = [
        pltpu.make_async_copy(vir_hbm, vir_ref, sems.at[0]),
        pltpu.make_async_copy(occ_hbm, occ_ref, sems.at[1]),
        pltpu.make_async_copy(occ_vec_hbm, occ_vec_ref, sems.at[2]),
    ]
    large = [
        pltpu.make_async_copy(amp_hbm.at[pl.ds(c, step)], amp_ref.at[pl.ds(c, step)], sems.at[3 + c // step])
        for c in range(0, cols, step)
    ]
    for copy in small + large:
        copy.start()
    for copy in small:
        copy.wait()
    me = lax.axis_index("col")
    first_a = lax.axis_index("row") * rows
    row_id = lax.broadcasted_iota(jnp.int32, (rows, occ), 0)
    a_labels = jnp.zeros((rows, occ), jnp.int32)
    for a in range(rows):
        a_labels = jnp.where(row_id == a, vir_ref[first_a + a], a_labels)
    if tables:
        label_tables(occ_ref, vir_ref, *tables)
    wanted = occ_ref[0] ^ occ_vec_ref[...] ^ a_labels
    for label in range(8):
        mask_ref[label] = jnp.where(wanted == label, 1.0, 0.0).astype(jnp.bfloat16)
    def run(col, i):
        start = col * cols
        lo, end = i * step, (i + 1) * step
        while lo < end:
            slot = (start + lo) % FOLD
            hi = min(end, lo + QUARTER - slot % QUARTER, FOLD if lo < FOLD else end)
            p = (slot // QUARTER) ^ col
            first = slot % QUARTER
            again = lo >= FOLD
            if p % 2 != odd:
                lo = hi
                continue

            def one(c, lo=lo, p=p, first=first, again=again):
                x = amp_ref[c] * mask_ref[vir_ref[start + c]]
                place = c - lo + first
                if again:
                    x = x + out_ref[p // 2, place]
                out_ref[p // 2, place] = x

            unit = 10
            whole = (hi - lo) // unit * unit

            def body(n, carry, lo=lo, one=one):
                for u in range(unit):
                    one(lo + n * unit + u)
                return carry

            lax.fori_loop(0, whole // unit, body, 0)
            for c in range(lo + whole, hi):
                one(c)
            lo = hi

    for i, copy in enumerate(large):
        copy.wait()
        for col in range(4):

            @pl.when(me == col)
            def _(col=col, i=i):
                run(col, i)


def turn_amplitudes(a_ref, b_ref, c_ref, out_ref, rows_ref, turned_ref):
    _, slots, rows, occ = a_ref.shape
    total = a_ref[0] + b_ref[0] + c_ref[...]
    rows_ref[...] = total.astype(jnp.float32).reshape(slots * rows, occ)
    half = occ // 2
    to = lax.broadcasted_iota(jnp.int32, (occ, occ), 0)
    frm = lax.broadcasted_iota(jnp.int32, (occ, occ), 1)
    pick = (frm == 2 * (to % half) + to // half).astype(jnp.bfloat16)
    for a in range(rows):
        block = rows_ref[pl.ds(a, slots, stride=rows), :].astype(jnp.bfloat16)
        turned = lax.dot_general(pick, block, (((1,), (1,)), ((), ())), preferred_element_type=jnp.float32)
        turned_ref[pl.ds(a, half, stride=rows), :] = jnp.concatenate([turned[:half], turned[half:]], axis=1)
    shift = own_shift()
    for i, member in enumerate(SAME):
        for d, partner in enumerate(PARTNERS):
            row = (member ^ partner) ^ shift
            out_ref[i, d] = turned_ref[pl.ds(pl.multiple_of(row * rows, rows), rows), :].astype(jnp.bfloat16)


def fold_integrals(int_hbm, lab_ref, vec_ref, after_hbm, out_ref, int_ref, sems):
    _, v, width = int_ref.shape
    step = v // sems.shape[1]
    copies = [
        [
            pltpu.make_async_copy(int_hbm.at[k, pl.ds(c, step)], int_ref.at[k, pl.ds(c, step)], sems.at[k, c // step])
            for c in range(0, v, step)
        ]
        for k in range(2)
    ]
    for copy in copies[0] + copies[1]:
        copy.start()
    for k in range(2):
        b_labels = vec_ref[k].astype(jnp.bfloat16)
        for i, copy in enumerate(copies[k]):
            copy.wait()
            for c in range(i * step, (i + 1) * step, 80):
                rows = slice(c, c + 80)
                c_labels = lab_ref[rows, :]
                for n in range(FOLD // 128):
                    total = None
                    for b in range(n * 128, width, FOLD):
                        size = min(128, width - b)
                        x = int_ref[k, rows, b : b + size]
                        x = jnp.where(c_labels[:, :size] == b_labels[:, b : b + size], x, jnp.zeros_like(x))
                        if size < 128:
                            x = jnp.concatenate([x, jnp.zeros((80, 128 - size), x.dtype)], axis=1)
                        total = x if total is None else total + x
                    out_ref[k, rows, n * 128 : (n + 1) * 128] = total
        out_ref[k, v:, :] = jnp.zeros((out_ref.shape[1] - v, FOLD), out_ref.dtype)


def contract(terms, last, *refs):
    quarters, partners = sorted({p for p, _ in terms}), sorted({d for _, d in terms})
    cut = len(quarters) + len(partners)
    t_refs, w_refs = refs[: len(quarters)], refs[len(quarters) : cut]
    lab_ref, tab_ref = refs[cut : cut + 2]
    sum_refs, (out_ref, a_lab_ref) = refs[cut + 2 : -2], refs[-2:]
    near, far, rows, lanes = t_refs[0].shape
    tall = w_refs[0].shape[1]
    me = lax.axis_index("col")
    shift = own_shift()
    for i, member in enumerate(SAME):
        label = lab_ref[pl.ds(pl.multiple_of((member ^ shift) * rows, rows), rows), :]
        a_lab_ref[i * rows : (i + 1) * rows, :] = label
    a_labels = a_lab_ref[...]
    total = sum_refs[0][...] if sum_refs else None
    blocks = [(p, d, t) for p, d in terms for t in range(tab_ref.shape[1] // 4)]
    for n in range(0, len(blocks), 2):
        lhs, w = [], []
        for p, d, t in blocks[n : n + 2]:
            block = 4 * t + (me ^ p)
            x = t_refs[quarters.index(p)][:, d].reshape(near * rows, lanes)
            c_labels = tab_ref[d, pl.ds(block, 1), :].astype(jnp.bfloat16)
            lhs.append(jnp.where(a_labels == c_labels, x, jnp.zeros_like(x)))
            c = pl.multiple_of(jnp.minimum(block * QUARTER, tall - QUARTER), QUARTER)
            w += [w_refs[partners.index(d)][k, pl.ds(c, QUARTER), :] for k in range(2)]
        lhs = lhs[0] if len(lhs) == 1 else jnp.concatenate(lhs, axis=1)
        part = jnp.dot(lhs, jnp.concatenate(w, axis=0), preferred_element_type=jnp.float32)
        total = part if total is None else total + part
    out_ref[...] = total * SEND_SCALE if last else total


def prepare(res_ref, vir_vec_ref, energy_vec_ref, occ_ref, vir_ref, occ_e_ref, vir_e_ref, plain_ref, factor_ref):
    rows, v = res_ref.shape
    first_a = lax.axis_index("row") * rows
    j = 1 + lax.axis_index("col")
    row_id = lax.broadcasted_iota(jnp.int32, (rows, 128), 0)
    a_labels = jnp.zeros((rows, 128), jnp.int32)
    a_energy = jnp.zeros((rows, 128), jnp.float32)
    for a in range(rows):
        a_labels = jnp.where(row_id == a, vir_ref[first_a + a], a_labels)
        a_energy = jnp.where(row_id == a, vir_e_ref[first_a + a], a_energy)
    b_labels = vir_vec_ref[0] ^ occ_ref[2 * lax.axis_index("row")] ^ occ_ref[0]
    for b in range(0, v, 128):
        width = min(128, v - b)
        at = slice(b, b + width)
        denominator = occ_e_ref[0] - a_energy[:, :width] + (occ_e_ref[j] - energy_vec_ref[:, at])
        plain_ref[:, at] = res_ref[:, at] / denominator
        factor_ref[:, at] = jnp.where(a_labels[:, :width] == b_labels[:, at], (1.0 / SEND_SCALE) / denominator, 0.0)


def finish(part_ref, plain_ref, factor_ref, out_ref):
    total = part_ref[...]
    v = out_ref.shape[1]
    for b in range(0, v, FOLD):
        width = min(FOLD, v - b)
        at = slice(b, b + width)
        out_ref[:, at] = plain_ref[:, at] + factor_ref[:, at] * total[:, :width]


def local(
    amplitudes,
    integrals,
    occupied_irrep,
    virtual_irrep,
    occupied_energy,
    virtual_energy,
    residual_in,
):
    o_win, rows, cols = amplitudes.shape
    occ_local, v, n_local = integrals.shape
    n_row = o_win // occ_local
    near = n_row // FAR
    smem = pl.BlockSpec(memory_space=pltpu.SMEM)
    vmem = pl.BlockSpec(memory_space=pltpu.VMEM)
    hbm = pl.BlockSpec(memory_space=pltpu.HBM)
    big = pltpu.CompilerParams(vmem_limit_bytes=24 * 1024 * 1024)
    occ_vec = occupied_irrep.reshape(1, o_win)

    chunks = 6
    def folded(odd, after, tables):
        return pl.pallas_call(
            functools.partial(fold_amplitudes, odd),
            out_shape=[jax.ShapeDtypeStruct((2, QUARTER, rows, o_win), jnp.bfloat16)] + tables,
            in_specs=[hbm] * 5,
            out_specs=[vmem] * (1 + len(tables)),
            scratch_shapes=[
                pltpu.VMEM((cols, rows, o_win), jnp.bfloat16),
                pltpu.VMEM((1, o_win), jnp.int32),
                pltpu.SMEM((o_win,), jnp.int32),
                pltpu.SMEM((v,), jnp.int32),
                pltpu.VMEM((8, rows, o_win), jnp.bfloat16),
                pltpu.SemaphoreType.DMA((3 + chunks,)),
            ],
            compiler_params=big,
            name="fold_amplitudes",
        )(
            pltpu.with_memory_space_constraint(amplitudes.transpose(2, 1, 0), pltpu.HBM),
            pltpu.with_memory_space_constraint(occ_vec, pltpu.HBM),
            pltpu.with_memory_space_constraint(occupied_irrep, pltpu.HBM),
            pltpu.with_memory_space_constraint(virtual_irrep, pltpu.HBM),
            after,
        )

    (send,) = folded(1, pltpu.with_memory_space_constraint(occupied_irrep, pltpu.HBM), [])
    tables = [
        jax.ShapeDtypeStruct((v, 128), jnp.bfloat16),
        jax.ShapeDtypeStruct((occ_local, 1, v), jnp.int32),
        jax.ShapeDtypeStruct((FAR, 4 * (-(-v // FOLD)), 2 * QUARTER), jnp.int32),
    ]
    keep, labels, vir_vecs, table = folded(0, send, tables)

    def swap(x, p):
        return lax.ppermute(x, "col", [(m, m ^ p) for m in range(4)])

    got = swap(send, 1)
    passed = keep[1] + got[1]
    w = pl.pallas_call(
        fold_integrals,
        out_shape=jax.ShapeDtypeStruct((occ_local, -(-v // QUARTER) * QUARTER, FOLD), jnp.bfloat16),
        in_specs=[hbm, vmem, vmem, hbm],
        out_specs=vmem,
        scratch_shapes=[
            pltpu.VMEM((occ_local, v, n_local), jnp.bfloat16),
            pltpu.SemaphoreType.DMA((occ_local, 5)),
        ],
        compiler_params=big,
        name="fold_integrals",
    )(pltpu.with_memory_space_constraint(integrals, pltpu.HBM), labels, vir_vecs, passed)
    far = swap(passed, 2)
    turned = pl.pallas_call(
        turn_amplitudes,
        out_shape=jax.ShapeDtypeStruct((near, FAR, rows, occ_local * QUARTER), jnp.bfloat16),
        in_specs=[vmem] * 3,
        out_specs=vmem,
        scratch_shapes=[
            pltpu.VMEM((QUARTER * rows, o_win), jnp.float32),
            pltpu.VMEM((n_row * rows, o_win), jnp.float32),
        ],
        compiler_params=big,
        cost_estimate=pl.CostEstimate(flops=4 * 10**10, bytes_accessed=10**6, transcendentals=0),
        name="turn_amplitudes",
    )(keep, got, far)
    classes = [[member ^ partner for member in SAME] for partner in PARTNERS]
    mine = lax.all_to_all(turned, "row", split_axis=0, concat_axis=0, tiled=True, axis_index_groups=classes)
    across = swap(mine, 2)

    gathered = [w, lax.ppermute(w, "row", [(r, r ^ PARTNERS[1]) for r in range(n_row)])]
    quarters = [mine, swap(mine, 1)]

    def contracted(terms, last, sums):
        used = [quarters[p] for p in sorted({p for p, _ in terms})] + [gathered[d] for d in sorted({d for _, d in terms})]
        return pl.pallas_call(
            functools.partial(contract, terms, last),
            out_shape=jax.ShapeDtypeStruct((near * rows, FOLD), jnp.float32),
            in_specs=[vmem] * (len(used) + 2 + len(sums)),
            out_specs=vmem,
            scratch_shapes=[pltpu.VMEM((near * rows, occ_local * QUARTER), jnp.bfloat16)],
            compiler_params=big,
            name="contract",
        )(*used, labels, table, *sums)

    partial = contracted([(0, 0)], False, [])
    across, partial = lax.optimization_barrier((across, partial))
    quarters += [across, swap(across, 1)]
    partial = contracted([(1, 0), (2, 0)], False, [partial])
    partial = contracted([(0, 1), (1, 1), (2, 1), (3, 0), (3, 1)], True, [partial])
    parts = lax.all_to_all(
        partial.astype(SEND_TYPE).reshape(near, rows, FOLD),
        "row",
        split_axis=0,
        concat_axis=0,
        tiled=True,
        axis_index_groups=classes,
    )
    plain, factor = pl.pallas_call(
        prepare,
        out_shape=[jax.ShapeDtypeStruct(residual_in.shape, jnp.float32)] * 2,
        in_specs=[vmem] * 3 + [smem] * 4,
        out_specs=[vmem, vmem],
        compiler_params=big,
        name="prepare",
    )(
        residual_in,
        vir_vecs,
        virtual_energy.reshape(1, v),
        occupied_irrep,
        virtual_irrep,
        occupied_energy,
        virtual_energy,
    )
    return pl.pallas_call(
        finish,
        out_shape=jax.ShapeDtypeStruct(residual_in.shape, jnp.float32),
        in_specs=[vmem] * 3,
        out_specs=vmem,
        compiler_params=big,
        name="finish",
    )(jnp.sum(parts.astype(jnp.float32), axis=0), plain, factor)


def solution(mesh):
    in_specs = (P(None, "row", "col"), P("row", None, "col"), P(), P(), P(), P(), P("row", "col"))
    out_specs = P("row", "col")
    return jax.shard_map(local, mesh=mesh, in_specs=in_specs, out_specs=out_specs, check_vma=False)
```

```python
import functools

import jax
import jax.numpy as jnp
from jax import lax
from jax.experimental import pallas as pl
from jax.experimental.pallas import tpu as pltpu
from jax.sharding import PartitionSpec as P

NJ = 4
FAR = 2
PARTNERS = (0, 48)
FOLD = 256
QUARTER = FOLD // 4
SEND_TYPE = jnp.float16
SEND_SCALE = 64.0


def colour(row):
    return (row >> 5) & 1


SAME = [row for row in range(64) if colour(row) == 0]


def own_shift():
    mine = colour(lax.axis_index("row"))
    shift = jnp.int32(0)
    for c in range(1, FAR):
        shift = jnp.where(mine == c, PARTNERS[c], shift)
    return shift


def fold_amplitudes(odd, amp_hbm, occ_vec_hbm, occ_hbm, vir_hbm, after_hbm, out_ref, amp_ref, occ_vec_ref, occ_ref, vir_ref, mask_ref, sems):
    cols, rows, occ = amp_ref.shape
    step = cols // (sems.shape[0] - 3)
    small = [
        pltpu.make_async_copy(vir_hbm, vir_ref, sems.at[0]),
        pltpu.make_async_copy(occ_hbm, occ_ref, sems.at[1]),
        pltpu.make_async_copy(occ_vec_hbm, occ_vec_ref, sems.at[2]),
    ]
    large = [
        pltpu.make_async_copy(amp_hbm.at[pl.ds(c, step)], amp_ref.at[pl.ds(c, step)], sems.at[3 + c // step])
        for c in range(0, cols, step)
    ]
    for copy in small + large:
        copy.start()
    for copy in small:
        copy.wait()
    me = lax.axis_index("col")
    first_a = lax.axis_index("row") * rows
    row_id = lax.broadcasted_iota(jnp.int32, (rows, occ), 0)
    a_labels = jnp.zeros((rows, occ), jnp.int32)
    for a in range(rows):
        a_labels = jnp.where(row_id == a, vir_ref[first_a + a], a_labels)
    wanted = occ_ref[0] ^ occ_vec_ref[...] ^ a_labels
    for label in range(8):
        mask_ref[label] = jnp.where(wanted == label, 1.0, 0.0).astype(jnp.bfloat16)
    def run(col, i):
        start = col * cols
        lo, end = i * step, (i + 1) * step
        while lo < end:
            slot = (start + lo) % FOLD
            hi = min(end, lo + QUARTER - slot % QUARTER, FOLD if lo < FOLD else end)
            p = (slot // QUARTER) ^ col
            first = slot % QUARTER
            again = lo >= FOLD
            if p % 2 != odd:
                lo = hi
                continue

            def one(c, lo=lo, p=p, first=first, again=again):
                x = amp_ref[c] * mask_ref[vir_ref[start + c]]
                place = c - lo + first
                if again:
                    x = x + out_ref[p // 2, place]
                out_ref[p // 2, place] = x

            unit = 10
            whole = (hi - lo) // unit * unit

            def body(n, carry, lo=lo, one=one):
                for u in range(unit):
                    one(lo + n * unit + u)
                return carry

            lax.fori_loop(0, whole // unit, body, 0)
            for c in range(lo + whole, hi):
                one(c)
            lo = hi

    for i, copy in enumerate(large):
        copy.wait()
        for col in range(4):

            @pl.when(me == col)
            def _(col=col, i=i):
                run(col, i)


def turn_amplitudes(a_ref, b_ref, c_ref, out_ref, rows_ref, turned_ref):
    _, slots, rows, occ = a_ref.shape
    total = a_ref[0] + b_ref[0] + c_ref[...]
    rows_ref[...] = total.astype(jnp.float32).reshape(slots * rows, occ)
    half = occ // 2
    to = lax.broadcasted_iota(jnp.int32, (occ, occ), 0)
    frm = lax.broadcasted_iota(jnp.int32, (occ, occ), 1)
    pick = (frm == 2 * (to % half) + to // half).astype(jnp.bfloat16)
    for a in range(rows):
        block = rows_ref[pl.ds(a, slots, stride=rows), :].astype(jnp.bfloat16)
        turned = lax.dot_general(pick, block, (((1,), (1,)), ((), ())), preferred_element_type=jnp.float32)
        turned_ref[pl.ds(a, half, stride=rows), :] = jnp.concatenate([turned[:half], turned[half:]], axis=1)
    shift = own_shift()
    for i, member in enumerate(SAME):
        for d, partner in enumerate(PARTNERS):
            row = (member ^ partner) ^ shift
            out_ref[i, d] = turned_ref[pl.ds(pl.multiple_of(row * rows, rows), rows), :].astype(jnp.bfloat16)


def fold_integrals(int_hbm, occ_hbm, vir_hbm, after_hbm, out_ref, lab_ref, vec_ref, tab_ref, int_ref, occ_ref, vir_ref, small, sems):
    _, v, width = int_ref.shape
    near = [pltpu.make_async_copy(vir_hbm, vir_ref, small.at[0]), pltpu.make_async_copy(occ_hbm, occ_ref, small.at[1])]
    step = v // sems.shape[1]
    copies = [
        [
            pltpu.make_async_copy(int_hbm.at[k, pl.ds(c, step)], int_ref.at[k, pl.ds(c, step)], sems.at[k, c // step])
            for c in range(0, v, step)
        ]
        for k in range(2)
    ]
    for copy in near + copies[0] + copies[1]:
        copy.start()
    for copy in near:
        copy.wait()
    begins = []
    for label in range(1, 8):
        lo, hi = jnp.int32(0), jnp.int32(v)
        for _ in range(v.bit_length()):
            mid = jnp.minimum((lo + hi) // 2, v - 1)
            reached = vir_ref[mid] >= label
            lo, hi = jnp.where(reached, lo, mid + 1), jnp.where(reached, mid, hi)
        begins.append(hi)

    def labels_of(orbital):
        return sum((orbital >= begin).astype(jnp.int32) for begin in begins)

    for c in range(0, v, 80):
        at = lax.broadcasted_iota(jnp.int32, (80, 128), 0) + c
        lab_ref[c : c + 80, :] = labels_of(at).astype(jnp.bfloat16)
    vir_vec = labels_of(lax.broadcasted_iota(jnp.int32, (1, width), 1))
    vec_ref[...] = vir_vec
    high = lax.broadcasted_iota(jnp.int32, (1, 2 * QUARTER), 1) >= QUARTER
    wanted = []
    for partner in PARTNERS:
        other = 2 * (lax.axis_index("row") ^ partner)
        wanted.append(jnp.where(high, occ_ref[other + 1], occ_ref[other]) ^ occ_ref[0])
    for block in range(tab_ref.shape[1]):
        size = min(QUARTER, v - block * QUARTER)
        x = jnp.full((1, QUARTER), 64, jnp.int32)
        if size > 0:
            x = vir_vec[:, block * QUARTER : block * QUARTER + size]
            if size < QUARTER:
                x = jnp.concatenate([jnp.full((1, QUARTER - size), 64, jnp.int32), x], axis=1)
        for d in range(FAR):
            tab_ref[d, block : block + 1, :] = jnp.concatenate([x, x], axis=1) ^ wanted[d]
    for k in range(2):
        label = occ_ref[lax.axis_index("row") * 2 + k] ^ occ_ref[1 + lax.axis_index("col")]
        b_labels = (vir_vec ^ label).astype(jnp.bfloat16)
        for i, copy in enumerate(copies[k]):
            copy.wait()
            for c in range(i * step, (i + 1) * step, 80):
                rows = slice(c, c + 80)
                c_labels = lab_ref[rows, :]
                for n in range(FOLD // 128):
                    total = None
                    for b in range(n * 128, width, FOLD):
                        size = min(128, width - b)
                        x = int_ref[k, rows, b : b + size]
                        x = jnp.where(c_labels[:, :size] == b_labels[:, b : b + size], x, jnp.zeros_like(x))
                        if size < 128:
                            x = jnp.concatenate([x, jnp.zeros((80, 128 - size), x.dtype)], axis=1)
                        total = x if total is None else total + x
                    out_ref[k, rows, n * 128 : (n + 1) * 128] = total


def contract(terms, last, *refs):
    quarters, partners = sorted({p for p, _ in terms}), sorted({d for _, d in terms})
    cut = len(quarters) + len(partners)
    t_refs, w_refs = refs[: len(quarters)], refs[len(quarters) : cut]
    lab_ref, tab_ref = refs[cut : cut + 2]
    sum_refs, (out_ref, a_lab_ref) = refs[cut + 2 : -2], refs[-2:]
    near, far, rows, lanes = t_refs[0].shape
    tall = w_refs[0].shape[1]
    me = lax.axis_index("col")
    shift = own_shift()
    for i, member in enumerate(SAME):
        label = lab_ref[pl.ds(pl.multiple_of((member ^ shift) * rows, rows), rows), :]
        a_lab_ref[i * rows : (i + 1) * rows, :] = label
    a_labels = a_lab_ref[...]
    total = sum_refs[0][...] if sum_refs else None
    blocks = [(p, d, t) for p, d in terms for t in range(tab_ref.shape[1] // 4)]
    for n in range(0, len(blocks), 2):
        lhs, w = [], []
        for p, d, t in blocks[n : n + 2]:
            block = 4 * t + (me ^ p)
            x = t_refs[quarters.index(p)][:, d].reshape(near * rows, lanes)
            if 4 * t * QUARTER + FOLD > tall:
                late = QUARTER - tall % QUARTER
                moved = jnp.concatenate([x[:, lanes - late :], x[:, : lanes - late]], axis=1)
                x = lax.select(block == tall // QUARTER, moved, x)
            c_labels = tab_ref[d, pl.ds(block, 1), :].astype(jnp.bfloat16)
            lhs.append(jnp.where(a_labels == c_labels, x, jnp.zeros_like(x)))
            c = pl.multiple_of(jnp.minimum(block * QUARTER, tall - QUARTER), QUARTER)
            w += [w_refs[partners.index(d)][k, pl.ds(c, QUARTER), :] for k in range(2)]
        lhs = lhs[0] if len(lhs) == 1 else jnp.concatenate(lhs, axis=1)
        part = jnp.dot(lhs, jnp.concatenate(w, axis=0), preferred_element_type=jnp.float32)
        total = part if total is None else total + part
    out_ref[...] = total * SEND_SCALE if last else total


def prepare(res_ref, vir_vec_ref, energy_vec_ref, occ_ref, vir_ref, occ_e_ref, vir_e_ref, plain_ref, factor_ref):
    rows, v = res_ref.shape
    first_a = lax.axis_index("row") * rows
    j = 1 + lax.axis_index("col")
    row_id = lax.broadcasted_iota(jnp.int32, (rows, 128), 0)
    a_labels = jnp.zeros((rows, 128), jnp.int32)
    a_energy = jnp.zeros((rows, 128), jnp.float32)
    for a in range(rows):
        a_labels = jnp.where(row_id == a, vir_ref[first_a + a], a_labels)
        a_energy = jnp.where(row_id == a, vir_e_ref[first_a + a], a_energy)
    b_labels = vir_vec_ref[...] ^ occ_ref[0] ^ occ_ref[j]
    for b in range(0, v, 128):
        width = min(128, v - b)
        at = slice(b, b + width)
        denominator = occ_e_ref[0] - a_energy[:, :width] + (occ_e_ref[j] - energy_vec_ref[:, at])
        plain_ref[:, at] = res_ref[:, at] / denominator
        factor_ref[:, at] = jnp.where(a_labels[:, :width] == b_labels[:, at], (1.0 / SEND_SCALE) / denominator, 0.0)


def finish(part_ref, plain_ref, factor_ref, out_ref):
    total = part_ref[...]
    v = out_ref.shape[1]
    for b in range(0, v, FOLD):
        width = min(FOLD, v - b)
        at = slice(b, b + width)
        out_ref[:, at] = plain_ref[:, at] + factor_ref[:, at] * total[:, :width]


def local(
    amplitudes,
    integrals,
    occupied_irrep,
    virtual_irrep,
    occupied_energy,
    virtual_energy,
    residual_in,
):
    o_win, rows, cols = amplitudes.shape
    occ_local, v, n_local = integrals.shape
    n_row = o_win // occ_local
    near = n_row // FAR
    smem = pl.BlockSpec(memory_space=pltpu.SMEM)
    vmem = pl.BlockSpec(memory_space=pltpu.VMEM)
    hbm = pl.BlockSpec(memory_space=pltpu.HBM)
    big = pltpu.CompilerParams(vmem_limit_bytes=24 * 1024 * 1024)
    occ_vec = occupied_irrep.reshape(1, o_win)

    chunks = 6
    def folded(odd, after):
        return pl.pallas_call(
            functools.partial(fold_amplitudes, odd),
            out_shape=jax.ShapeDtypeStruct((2, QUARTER, rows, o_win), jnp.bfloat16),
            in_specs=[hbm] * 5,
            out_specs=vmem,
            scratch_shapes=[
                pltpu.VMEM((cols, rows, o_win), jnp.bfloat16),
                pltpu.VMEM((1, o_win), jnp.int32),
                pltpu.SMEM((o_win,), jnp.int32),
                pltpu.SMEM((v,), jnp.int32),
                pltpu.VMEM((8, rows, o_win), jnp.bfloat16),
                pltpu.SemaphoreType.DMA((3 + chunks,)),
            ],
            compiler_params=big,
            name="fold_amplitudes",
        )(
            pltpu.with_memory_space_constraint(amplitudes.transpose(2, 1, 0), pltpu.HBM),
            pltpu.with_memory_space_constraint(occ_vec, pltpu.HBM),
            pltpu.with_memory_space_constraint(occupied_irrep, pltpu.HBM),
            pltpu.with_memory_space_constraint(virtual_irrep, pltpu.HBM),
            after,
        )

    send = folded(1, pltpu.with_memory_space_constraint(occupied_irrep, pltpu.HBM))
    keep = folded(0, send)

    def swap(x, p):
        return lax.ppermute(x, "col", [(m, m ^ p) for m in range(4)])

    got = swap(send, 1)
    passed = keep[1] + got[1]
    w, labels, vir_vec, table = pl.pallas_call(
        fold_integrals,
        out_shape=[
            jax.ShapeDtypeStruct((occ_local, v, FOLD), jnp.bfloat16),
            jax.ShapeDtypeStruct((v, 128), jnp.bfloat16),
            jax.ShapeDtypeStruct((1, v), jnp.int32),
            jax.ShapeDtypeStruct((FAR, 4 * (-(-v // FOLD)), 2 * QUARTER), jnp.int32),
        ],
        in_specs=[hbm] * 4,
        out_specs=[vmem] * 4,
        scratch_shapes=[
            pltpu.VMEM((occ_local, v, n_local), jnp.bfloat16),
            pltpu.SMEM((o_win,), jnp.int32),
            pltpu.SMEM((v,), jnp.int32),
            pltpu.SemaphoreType.DMA((2,)),
            pltpu.SemaphoreType.DMA((occ_local, 5)),
        ],
        compiler_params=big,
        name="fold_integrals",
    )(
        pltpu.with_memory_space_constraint(integrals, pltpu.HBM),
        pltpu.with_memory_space_constraint(occupied_irrep, pltpu.HBM),
        pltpu.with_memory_space_constraint(virtual_irrep, pltpu.HBM),
        passed,
    )
    far = swap(passed, 2)
    turned = pl.pallas_call(
        turn_amplitudes,
        out_shape=jax.ShapeDtypeStruct((near, FAR, rows, occ_local * QUARTER), jnp.bfloat16),
        in_specs=[vmem] * 3,
        out_specs=vmem,
        scratch_shapes=[
            pltpu.VMEM((QUARTER * rows, o_win), jnp.float32),
            pltpu.VMEM((n_row * rows, o_win), jnp.float32),
        ],
        compiler_params=big,
        cost_estimate=pl.CostEstimate(flops=4 * 10**10, bytes_accessed=10**6, transcendentals=0),
        name="turn_amplitudes",
    )(keep, got, far)
    classes = [[member ^ partner for member in SAME] for partner in PARTNERS]
    mine = lax.all_to_all(turned, "row", split_axis=0, concat_axis=0, tiled=True, axis_index_groups=classes)
    across = swap(mine, 2)

    gathered = [w, lax.ppermute(w, "row", [(r, r ^ PARTNERS[1]) for r in range(n_row)])]
    quarters = [mine, swap(mine, 1)]

    def contracted(terms, last, sums):
        used = [quarters[p] for p in sorted({p for p, _ in terms})] + [gathered[d] for d in sorted({d for _, d in terms})]
        return pl.pallas_call(
            functools.partial(contract, terms, last),
            out_shape=jax.ShapeDtypeStruct((near * rows, FOLD), jnp.float32),
            in_specs=[vmem] * (len(used) + 2 + len(sums)),
            out_specs=vmem,
            scratch_shapes=[pltpu.VMEM((near * rows, occ_local * QUARTER), jnp.bfloat16)],
            compiler_params=big,
            name="contract",
        )(*used, labels, table, *sums)

    partial = contracted([(0, 0)], False, [])
    across, partial = lax.optimization_barrier((across, partial))
    quarters += [across, swap(across, 1)]
    partial = contracted([(1, 0), (2, 0)], False, [partial])
    partial = contracted([(0, 1), (1, 1), (2, 1), (3, 0), (3, 1)], True, [partial])
    parts = lax.all_to_all(
        partial.astype(SEND_TYPE).reshape(near, rows, FOLD),
        "row",
        split_axis=0,
        concat_axis=0,
        tiled=True,
        axis_index_groups=classes,
    )
    plain, factor = pl.pallas_call(
        prepare,
        out_shape=[jax.ShapeDtypeStruct(residual_in.shape, jnp.float32)] * 2,
        in_specs=[vmem] * 3 + [smem] * 4,
        out_specs=[vmem, vmem],
        compiler_params=big,
        name="prepare",
    )(
        residual_in,
        vir_vec,
        virtual_energy.reshape(1, v),
        occupied_irrep,
        virtual_irrep,
        occupied_energy,
        virtual_energy,
    )
    return pl.pallas_call(
        finish,
        out_shape=jax.ShapeDtypeStruct(residual_in.shape, jnp.float32),
        in_specs=[vmem] * 3,
        out_specs=vmem,
        compiler_params=big,
        name="finish",
    )(jnp.sum(parts.astype(jnp.float32), axis=0), plain, factor)


def solution(mesh):
    in_specs = (P(None, "row", "col"), P("row", None, "col"), P(), P(), P(), P(), P("row", "col"))
    out_specs = P("row", "col")
    return jax.shard_map(local, mesh=mesh, in_specs=in_specs, out_specs=out_specs, check_vma=False)
```
